32 devices in a mesh: snap: 8 (over z, x), vert: 4 (over y, core).
Axes of the slice: x: 2, y: 2, z: 4, core: 2. Of those that a mesh axis runs over, the one named last changes fastest.
Arguments:
- features: bfloat16 [8, 1024, 512], P('snap', 'vert'), may hold values from -6 to 6
- tile_values: bfloat16 [8, 8, 12, 128, 128], P('snap', 'vert'), may hold values from -0.21875 to 0.21875
- tile_column: int32 [8, 8, 12], P('snap', 'vert'), may hold values from 0 to 7
- tile_count: int32 [8, 8], P('snap', 'vert'), may hold values from 1 to 12, 48 in all within a row
- message_one: bfloat16 [512, 512], replicated, may hold values from -0.25 to 0.25
- root_one: bfloat16 [512, 512], replicated, may hold values from -0.25 to 0.25
- time_taps: float32 [16, 512], replicated, may hold values from -1.5 to 1.5
- message_two: bfloat16 [512, 512], replicated, may hold values from -0.25 to 0.25
- root_two: bfloat16 [512, 512], replicated, may hold values from -0.25 to 0.25
Outputs:
- embedding: bfloat16 [8, 1024, 512], P('snap', 'vert')
The draws below stay inside these ranges and needn't reach their ends.
Inputs may be any that keep to these rules, and one draw needn't show every extreme that they name: `tile_count`: over one snapshot the counts sum to 48, and some row block has 12 live slots; slots at or past the count are ignored. `tile_column`: blocks may repeat within a row block's list.
All inputs are finite; a program needn't handle non-finite values.
Results may differ from the reference program's by a relative error of at most 0.0064.
Values may be sent and summed in bfloat16 or wider, within the bound.
A program may use at most 64 MiB of HBM per device.

```python
import math
import jax
import jax.numpy as jnp
import numpy as np
from jax import lax

WIDTH = 512
TILE = 128
SLOTS = 12
TAPS = 16
SNAPS = 8
BLOCKS = 8
VERTS = 1024


def touch_ends(entries, rng, least, high):
    shape = entries.shape
    spot = [jax.random.randint(jax.random.fold_in(rng, axis), (), 0, shape[axis]) for axis in range(len(shape))]
    entries = entries.at[tuple(spot)].set(least)
    longest = shape.index(max(shape))
    spot[longest] = (spot[longest] + 1) % shape[longest]
    return entries.at[tuple(spot)].set(high)


def levels(rng, dims, split, smallest, top_value):
    def one(position, shards_of):
        draws = jax.random.uniform(jax.random.fold_in(jax.random.fold_in(rng, 6), position), (shards_of,), jnp.float32, smallest / len(split), top_value / len(split))
        return jnp.repeat(jnp.exp(draws), dims[position] // shards_of).reshape((-1,) + (1,) * (len(dims) - position - 1))

    level = one(*split[0])
    for cut in split[1:]:
        level = level * one(*cut)
    return level


def profile(amount, total, reach, skew):
    portions = [(1 << 20) // math.isqrt(standing ** skew) + 1 for standing in range(2, amount + 1)]
    rest, holding = total - reach - (amount - 1), [1] * (amount - 1)
    while rest > 0:
        free = [i for i in range(amount - 1) if holding[i] < reach]
        whole, budget = sum([portions[i] for i in free]), rest
        for i in free:
            extra = min(reach - holding[i], max(1, budget * portions[i] // whole), rest)
            holding[i] = holding[i] + extra
            rest = rest - extra
    return np.array([reach] + holding)


def uneven(stream_key, number_of, total, reach, lean):
    if number_of == 2:
        one = jax.random.randint(stream_key, (), max(1, total - reach), min(reach, total - 1) + 1)
        return jnp.stack([one, total - one])
    sizes = jnp.asarray(profile(number_of, total, reach, lean), jnp.int32)
    pairs = (number_of - 1) // 2
    donor, sink = sizes[1:1 + 2 * pairs:2], sizes[2:2 + 2 * pairs:2]
    slack = jnp.minimum(donor - 1, reach - sink)
    moved = jax.random.randint(jax.random.fold_in(stream_key, 1), (pairs,), 0, 1 << 20) % (slack + 1)
    sizes = sizes.at[1:1 + 2 * pairs:2].set(donor - moved).at[2:2 + 2 * pairs:2].set(sink + moved)
    return sizes[jax.random.permutation(jax.random.fold_in(stream_key, 2), number_of)]


def gaussian(rng, dims, width, most, shards=(), kind=jnp.bfloat16):
    values = jax.random.normal(rng, dims, jnp.float32) * width
    if len(shards) > 0:
        values = levels(rng, dims, shards, -0.22, 0.18) * values
    return jnp.clip(values, min=-most, max=most).astype(kind)


def setup_inputs(seed: int = 0) -> dict:
    arg_keys = jax.random.split(jax.random.key(seed), 10)
    return {
        "features": gaussian(arg_keys[0], (SNAPS, VERTS, WIDTH), 1.0, 6.0, ((0, 8), (1, 4))),
        "tile_values": gaussian(arg_keys[1], (SNAPS, BLOCKS, SLOTS, TILE, TILE), (TILE * SLOTS // 2) ** -0.5, 0.21875, ((0, 8), (1, 4))),
        "tile_column": touch_ends(jax.random.randint(arg_keys[2], (SNAPS, BLOCKS, SLOTS), 0, BLOCKS), jax.random.fold_in(arg_keys[2], 1), 0, BLOCKS - 1).astype(jnp.int32),
        "tile_count": jax.vmap(lambda own: uneven(own, BLOCKS, BLOCKS * SLOTS // 2, SLOTS, 2))(jax.random.split(arg_keys[3], SNAPS)).reshape((SNAPS, BLOCKS)).astype(jnp.int32),
        "message_one": gaussian(arg_keys[4], (WIDTH, WIDTH), WIDTH ** -0.5, 0.25),
        "root_one": gaussian(arg_keys[5], (WIDTH, WIDTH), WIDTH ** -0.5, 0.25),
        "time_taps": gaussian(arg_keys[6], (TAPS, WIDTH), 0.25, 1.5, (), jnp.float32),
        "message_two": gaussian(arg_keys[7], (WIDTH, WIDTH), WIDTH ** -0.5, 0.25),
        "root_two": gaussian(arg_keys[8], (WIDTH, WIDTH), WIDTH ** -0.5, 0.25),
    }


def graph_layer(inputs, tiles, columns, counts, w_message, w_root):
    messages = jnp.dot(inputs, w_message, preferred_element_type=jnp.float32).astype(jnp.bfloat16)
    blocks = messages.astype(jnp.float32).reshape(BLOCKS, TILE, WIDTH)
    live = (jnp.arange(SLOTS, dtype=jnp.int32)[None, :] < counts[:, None]).astype(jnp.float32)
    picked = blocks[columns.astype(jnp.int32)] * live[:, :, None, None]
    summed = jnp.einsum('rkij,rkjf->rif', tiles.astype(jnp.float32), picked).reshape(VERTS, WIDTH)
    total = summed + jnp.dot(inputs, w_root, preferred_element_type=jnp.float32)
    return jnp.maximum(total, 0.0).astype(jnp.bfloat16)


def reference(features, tile_values, tile_column, tile_count, message_one, root_one, time_taps, message_two, root_two):
    hidden = lax.map(lambda item: graph_layer(item[0], item[1], item[2], item[3], message_one, root_one),
                     (features, tile_values, tile_column, tile_count))
    wide = hidden.astype(jnp.float32)
    padded = jnp.concatenate([jnp.zeros((TAPS - 1, VERTS, WIDTH), jnp.float32), wide], 0)
    mixed = jnp.zeros((SNAPS, VERTS, WIDTH), jnp.float32)
    for offset in range(TAPS):
        mixed = mixed + time_taps[offset][None, None, :] * padded[TAPS - 1 - offset:TAPS - 1 - offset + SNAPS]
    mixed = mixed.astype(jnp.bfloat16)
    return lax.map(lambda item: graph_layer(item[0], item[1], item[2], item[3], message_two, root_two),
                   (mixed, tile_values, tile_column, tile_count))
```

```python
import functools

import jax
import jax.numpy as jnp
from jax import lax
from jax.experimental import pallas as pl
from jax.experimental.pallas import tpu as pltpu
from jax.sharding import PartitionSpec as P

MESH = pl.DeviceIdType.MESH
HALVES = 2
GROUPS = 2
CHUNKS = 4
F32 = jnp.float32
BF16 = jnp.bfloat16


def flip(index, mask):
    out, bit = index, 1
    while bit <= mask:
        if mask & bit:
            out = out + (1 - 2 * ((index // bit) % 2)) * bit
        bit *= 2
    return out


def kernel(
    sizes,
    features,
    tile_values,
    columns,
    counts,
    message_one,
    root_one,
    time_taps,
    message_two,
    root_two,
    out,
    feats,
    tiles,
    dense,
    weights,
    taps,
    acc,
    total,
    hid,
    by_time,
    mix,
    mixed,
    local_sem,
    near_sem,
    y1_send,
    y1_recv,
    f1_send,
    f1_recv,
    p2_send,
    p2_recv,
    p3_send,
    p3_recv,
    y4_send,
    y4_recv,
    s4_send,
    s4_recv,
    f4_send,
    f4_recv,
):
    n, nv, rows, width, slots, tile = sizes
    ny = nv // 2
    per = rows // tile
    cols = width // HALVES
    piece_rows = max(rows // n, 16)
    across = n // (rows // piece_rows)
    piece_cols = cols // across
    me_s, me_v = lax.axis_index("snap"), lax.axis_index("vert")
    y, core = me_v // 2, me_v % 2
    sib = y * 2 + 1 - core

    def piece(p):
        r = pl.multiple_of((p // across) * piece_rows, piece_rows)
        if across == 1:
            return pl.ds(r, piece_rows), slice(0, piece_cols)
        return pl.ds(r, piece_rows), pl.ds(pl.multiple_of((p % across) * piece_cols, piece_cols), piece_cols)

    def remote(src, dst, send, recv, s, v):
        return pltpu.make_async_remote_copy(
            src_ref=src, dst_ref=dst, send_sem=send, recv_sem=recv, device_id=(s, v), device_id_type=MESH
        )

    sent = []

    def go(*args):
        copy = remote(*args)
        copy.start()
        sent.append(copy)

    def y_to(d):
        return ((y + d) % ny) * 2 + core

    def y_from(d):
        return ((y - d + ny) % ny) * 2 + core

    own_feats = pltpu.make_async_copy(features.at[0], feats.at[me_v], local_sem.at[0])
    load_tiles = pltpu.make_async_copy(tile_values.at[0], tiles, local_sem.at[1])
    loads = [
        pltpu.make_async_copy(ref, weights.at[i], local_sem.at[2 + i])
        for i, ref in enumerate((root_one, message_one, root_two, message_two))
    ]
    load_taps = pltpu.make_async_copy(time_taps, taps, local_sem.at[6])
    load_tiles.start()
    own_feats.start()
    for load in loads:
        load.start()
    load_taps.start()

    barrier = pltpu.get_barrier_semaphore()
    for d in range(1, n):
        pl.semaphore_signal(barrier, inc=1, device_id=(flip(me_s, d), me_v), device_id_type=MESH)
    for d in range(1, ny):
        pl.semaphore_signal(barrier, inc=1, device_id=(me_s, y_to(d)), device_id_type=MESH)
    pl.semaphore_signal(barrier, inc=1, device_id=(me_s, sib), device_id_type=MESH)
    pl.semaphore_wait(barrier, n - 1 + ny)

    step = rows // CHUNKS
    for q in range(CHUNKS):
        part = pl.ds(q * step, step)
        for d in range(1, ny):
            go(features.at[0, part], feats.at[me_v, part], y1_send.at[d, q], y1_recv.at[d, q], me_s, y_to(d))
    go(features.at[0], feats.at[me_v], near_sem.at[0], near_sem.at[1], me_s, sib)

    def pass_on(q):
        part = pl.ds(q * step, step)
        for d in range(1, ny):
            src = y_from(d)
            block = feats.at[src, part]
            remote(block, block, y1_send.at[d, q], y1_recv.at[d, q], me_s, src).wait_recv()
            go(block, block, f1_send.at[d, q], f1_recv.at[d, q], me_s, sib)

    load_tiles.wait()
    live = [
        [jnp.where(k < counts[0, b], columns[0, b, k], -1) for k in range(slots)] for b in range(per)
    ]

    def fill(v, carry):
        for b in range(per):
            for j in range(per):
                block = jnp.zeros((tile, tile), F32)
                for k in range(slots):
                    scale = jnp.where(live[b][k] == v * per + j, 1.0, 0.0).astype(F32)
                    block = block + scale * tiles[b, k].astype(F32)
                dense[v, b * tile : (b + 1) * tile, j * tile : (j + 1) * tile] = block.astype(BF16)
        return carry

    lax.fori_loop(0, nv, fill, 0)

    def dot(a, b):
        return jnp.dot(a, b, preferred_element_type=F32)

    pass_on(0)
    own_feats.wait()
    loads[0].wait()
    total[...] = dot(feats[me_v], weights[0])
    pass_on(1)
    acc[...] = dot(dense[me_v], feats[me_v])
    for q in range(2, CHUNKS):
        pass_on(q)
    block = feats.at[sib]
    remote(block, block, near_sem.at[0], near_sem.at[1], me_s, sib).wait_recv()
    acc[...] += dot(dense[sib], feats[sib])
    for d in range(1, ny):
        src = y_from(d)
        acc[...] += dot(dense[src], feats[src])
    for d in range(1, ny):
        src = ((y - d + ny) % ny) * 2 + 1 - core
        for q in range(CHUNKS):
            block = feats.at[src, pl.ds(q * step, step)]
            remote(block, block, f1_send.at[d, q], f1_recv.at[d, q], me_s, sib).wait_recv()
        acc[...] += dot(dense[src], feats[src])

    loads[1].wait()
    order = list(range(n // 2, n)) + list(range(1, n // 2))
    near = acc[...].astype(BF16)
    for h in range(HALVES):
        lanes = slice(h * cols, (h + 1) * cols)
        value = total[:, lanes] + dot(near, weights[1, :, lanes])
        hid[h] = jnp.maximum(value, 0.0).astype(BF16)
        for d in order:
            p = flip(me_s, d)
            r, c = piece(p)
            go(hid.at[h, r, c], by_time.at[h, me_s], p2_send.at[h, d], p2_recv.at[h, d], p, me_v)

    load_taps.wait()
    for h in range(HALVES):
        r, c = piece(me_s)
        by_time[h, me_s] = hid[h, r, c]
        for d in range(1, n):
            p = flip(me_s, d)
            block = by_time.at[h, p]
            remote(block, block, p2_send.at[h, d], p2_recv.at[h, d], p, me_v).wait_recv()
        shift = 0 if across == 1 else (me_s % across) * piece_cols
        for i in range(0, piece_rows, 16):
            for j in range(0, piece_cols, 128):
                at = h * cols + j + shift
                if across > 1:
                    at = pl.multiple_of(at, 128)
                filt = taps[:, pl.ds(at, 128)]
                wide = [by_time[h, t, i : i + 16, j : j + 128].astype(F32) for t in range(n)]
                for t in range(n):
                    value = filt[0:1] * wide[t]
                    for k in range(1, min(filt.shape[0] - 1, t) + 1):
                        value = value + filt[k : k + 1] * wide[t - k]
                    mix[h, t, i : i + 16, j : j + 128] = value.astype(BF16)
        for d in order:
            p = flip(me_s, d)
            go(mix.at[h, p], mixed.at[h, me_v, r, c], p3_send.at[h, d], p3_recv.at[h, d], p, me_v)
        mixed[h, me_v, r, c] = mix[h, me_s]

    half = rows // GROUPS
    size = n // GROUPS

    def group_rows(g):
        start = me_s // size if g == 0 else 1 - me_s // size
        return pl.ds(pl.multiple_of(start * half, half), half)

    def send_group(h, g):
        for d in range(g * size, (g + 1) * size):
            if d > 0:
                p = flip(me_s, d)
                r, c = piece(p)
                block = mixed.at[h, me_v, r, c]
                remote(block, block, p3_send.at[h, d], p3_recv.at[h, d], p, me_v).wait_recv()
        block = mixed.at[h, me_v, group_rows(g)]
        for d in range(1, ny):
            go(block, block, y4_send.at[d, h, g], y4_recv.at[d, h, g], me_s, y_to(d))
        go(block, block, s4_send.at[h, g], s4_recv.at[h, g], me_s, sib)

    def pass_group(h, g):
        for d in range(1, ny):
            src = y_from(d)
            block = mixed.at[h, src, group_rows(g)]
            remote(block, block, y4_send.at[d, h, g], y4_recv.at[d, h, g], me_s, src).wait_recv()
            go(block, block, f4_send.at[d, h, g], f4_recv.at[d, h, g], me_s, sib)

    def near_part(h):
        lanes = slice(h * cols, (h + 1) * cols)
        acc[:, lanes] = dot(dense[me_v], mixed[h, me_v])
        for g in range(GROUPS):
            block = mixed.at[h, sib, group_rows(g)]
            remote(block, block, s4_send.at[h, g], s4_recv.at[h, g], me_s, sib).wait_recv()
        acc[:, lanes] += dot(dense[sib], mixed[h, sib])
        own = dot(mixed[h, me_v], weights[2, lanes, :])
        if h == 0:
            total[...] = own
        else:
            total[...] += own

    def far_part(h):
        lanes = slice(h * cols, (h + 1) * cols)
        for d in range(1, ny):
            src = y_from(d)
            acc[:, lanes] += dot(dense[src], mixed[h, src])
        for d in range(1, ny):
            src = ((y - d + ny) % ny) * 2 + 1 - core
            for g in range(GROUPS):
                block = mixed.at[h, src, group_rows(g)]
                remote(block, block, f4_send.at[d, h, g], f4_recv.at[d, h, g], me_s, sib).wait_recv()
            acc[:, lanes] += dot(dense[src], mixed[h, src])
        total[...] += dot(acc[:, lanes].astype(BF16), weights[3, lanes, :])

    loads[2].wait()
    loads[3].wait()
    send_group(0, 0)
    send_group(0, 1)
    pass_group(0, 0)
    send_group(1, 0)
    pass_group(0, 1)
    near_part(0)
    send_group(1, 1)
    pass_group(1, 0)
    far_part(0)
    pass_group(1, 1)
    near_part(1)
    far_part(1)
    out[0] = jnp.maximum(total[...], 0.0).astype(BF16)
    for copy in sent:
        copy.wait_send()


def shards(n, nv, features, tile_values, tile_column, tile_count, *rest):
    _, rows, width = features.shape
    _, per, slots, tile, _ = tile_values.shape
    ny = nv // 2
    cols = width // HALVES
    piece_rows = max(rows // n, 16)
    piece_cols = cols // (n // (rows // piece_rows))
    taps = rest[2].shape[0]
    dma = pltpu.SemaphoreType.DMA
    hbm = pl.BlockSpec(memory_space=pl.ANY)
    smem = pl.BlockSpec(memory_space=pltpu.SMEM)
    return pl.pallas_call(
        functools.partial(kernel, (n, nv, rows, width, slots, tile)),
        out_shape=jax.ShapeDtypeStruct((1, rows, width), BF16),
        in_specs=[hbm, hbm, smem, smem] + [hbm] * 5,
        out_specs=pl.BlockSpec(memory_space=pltpu.VMEM),
        scratch_shapes=[
            pltpu.VMEM((nv, rows, width), BF16),
            pltpu.VMEM((per, slots, tile, tile), BF16),
            pltpu.VMEM((nv, rows, rows), BF16),
            pltpu.VMEM((4, width, width), BF16),
            pltpu.VMEM((taps, width), F32),
            pltpu.VMEM((rows, width), F32),
            pltpu.VMEM((rows, width), F32),
            pltpu.VMEM((HALVES, rows, cols), BF16),
            pltpu.VMEM((HALVES, n, piece_rows, piece_cols), BF16),
            pltpu.VMEM((HALVES, n, piece_rows, piece_cols), BF16),
            pltpu.VMEM((HALVES, nv, rows, cols), BF16),
            dma((7,)),
            dma((2,)),
            dma((ny, CHUNKS)),
            dma((ny, CHUNKS)),
            dma((ny, CHUNKS)),
            dma((ny, CHUNKS)),
            dma((HALVES, n)),
            dma((HALVES, n)),
            dma((HALVES, n)),
            dma((HALVES, n)),
            dma((ny, HALVES, GROUPS)),
            dma((ny, HALVES, GROUPS)),
            dma((HALVES, GROUPS)),
            dma((HALVES, GROUPS)),
            dma((ny, HALVES, GROUPS)),
            dma((ny, HALVES, GROUPS)),
        ],
        compiler_params=pltpu.CompilerParams(
            collective_id=0, has_side_effects=True, vmem_limit_bytes=40 * 1024 * 1024
        ),
    )(features, tile_values, tile_column, tile_count, *rest)


def solution(mesh):
    n, nv = mesh.shape["snap"], mesh.shape["vert"]
    return jax.shard_map(
        functools.partial(shards, n, nv),
        mesh=mesh,
        in_specs=(
            P("snap", "vert", None),
            P("snap", "vert", None, None, None),
            P("snap", "vert", None),
            P("snap", "vert"),
            P(),
            P(),
            P(),
            P(),
            P(),
        ),
        out_specs=P("snap", "vert", None),
        check_vma=False,
    )
```

```python
import functools

import jax
import jax.numpy as jnp
from jax import lax
from jax.experimental import pallas as pl
from jax.experimental.pallas import tpu as pltpu
from jax.sharding import PartitionSpec as P

MESH = pl.DeviceIdType.MESH
HALVES = 2
GROUPS = 2
CHUNKS = 4
F32 = jnp.float32
BF16 = jnp.bfloat16


def flip(index, mask):
    out, bit = index, 1
    while bit <= mask:
        if mask & bit:
            out = out + (1 - 2 * ((index // bit) % 2)) * bit
        bit *= 2
    return out


def kernel(
    sizes,
    features,
    tile_values,
    columns,
    counts,
    message_one,
    root_one,
    time_taps,
    message_two,
    root_two,
    out,
    column_smem,
    count_smem,
    feats,
    tiles,
    dense,
    weights,
    taps,
    acc,
    total,
    hid,
    by_time,
    mix,
    mixed,
    local_sem,
    near_sem,
    y1_send,
    y1_recv,
    f1_send,
    f1_recv,
    p2_send,
    p2_recv,
    p3_send,
    p3_recv,
    y4_send,
    y4_recv,
    s4_send,
    s4_recv,
    f4_send,
    f4_recv,
):
    n, nv, rows, width, slots, tile = sizes
    ny = nv // 2
    per = rows // tile
    cols = width // HALVES
    piece_rows = max(rows // n, 16)
    across = n // (rows // piece_rows)
    piece_cols = cols // across
    me_s, me_v = lax.axis_index("snap"), lax.axis_index("vert")
    y, core = me_v // 2, me_v % 2
    sib = y * 2 + 1 - core

    def piece(p):
        r = pl.multiple_of((p // across) * piece_rows, piece_rows)
        if across == 1:
            return pl.ds(r, piece_rows), slice(0, piece_cols)
        return pl.ds(r, piece_rows), pl.ds(pl.multiple_of((p % across) * piece_cols, piece_cols), piece_cols)

    def remote(src, dst, send, recv, s, v):
        return pltpu.make_async_remote_copy(
            src_ref=src, dst_ref=dst, send_sem=send, recv_sem=recv, device_id=(s, v), device_id_type=MESH
        )

    sent = []

    def go(*args):
        copy = remote(*args)
        copy.start()
        sent.append(copy)

    def y_to(d):
        return ((y + d) % ny) * 2 + core

    def y_from(d):
        return ((y - d + ny) % ny) * 2 + core

    own_feats = pltpu.make_async_copy(features.at[0], feats.at[me_v], local_sem.at[0])
    load_tiles = pltpu.make_async_copy(tile_values.at[0], tiles, local_sem.at[1])
    loads = [
        pltpu.make_async_copy(ref, weights.at[i], local_sem.at[2 + i])
        for i, ref in enumerate((root_one, message_one, root_two, message_two))
    ]
    load_taps = pltpu.make_async_copy(time_taps, taps, local_sem.at[6])
    load_columns = pltpu.make_async_copy(columns.at[0], column_smem, local_sem.at[7])
    load_counts = pltpu.make_async_copy(counts, count_smem, local_sem.at[8])
    load_columns.start()
    load_counts.start()
    load_tiles.start()
    own_feats.start()
    for load in loads:
        load.start()
    load_taps.start()

    barrier = pltpu.get_barrier_semaphore()
    for d in range(1, n):
        pl.semaphore_signal(barrier, inc=1, device_id=(flip(me_s, d), me_v), device_id_type=MESH)
    for d in range(1, ny):
        pl.semaphore_signal(barrier, inc=1, device_id=(me_s, y_to(d)), device_id_type=MESH)
    pl.semaphore_signal(barrier, inc=1, device_id=(me_s, sib), device_id_type=MESH)
    pl.semaphore_wait(barrier, n - 1 + ny)

    step = rows // CHUNKS
    for q in range(CHUNKS):
        part = pl.ds(q * step, step)
        for d in range(1, ny):
            go(features.at[0, part], feats.at[me_v, part], y1_send.at[d, q], y1_recv.at[d, q], me_s, y_to(d))
    go(features.at[0], feats.at[me_v], near_sem.at[0], near_sem.at[1], me_s, sib)

    def pass_on(q):
        part = pl.ds(q * step, step)
        for d in range(1, ny):
            src = y_from(d)
            block = feats.at[src, part]
            remote(block, block, y1_send.at[d, q], y1_recv.at[d, q], me_s, src).wait_recv()
            go(block, block, f1_send.at[d, q], f1_recv.at[d, q], me_s, sib)

    load_columns.wait()
    load_counts.wait()
    load_tiles.wait()
    live = [
        [jnp.where(k < count_smem[0, b], column_smem[b, k], -1) for k in range(slots)] for b in range(per)
    ]

    def fill(v, carry):
        for b in range(per):
            for j in range(per):
                block = jnp.zeros((tile, tile), F32)
                for k in range(slots):
                    scale = jnp.where(live[b][k] == v * per + j, 1.0, 0.0).astype(F32)
                    block = block + scale * tiles[b, k].astype(F32)
                dense[v, b * tile : (b + 1) * tile, j * tile : (j + 1) * tile] = block.astype(BF16)
        return carry

    lax.fori_loop(0, nv, fill, 0)

    def dot(a, b):
        return jnp.dot(a, b, preferred_element_type=F32)

    pass_on(0)
    own_feats.wait()
    loads[0].wait()
    total[...] = dot(feats[me_v], weights[0])
    pass_on(1)
    acc[...] = dot(dense[me_v], feats[me_v])
    for q in range(2, CHUNKS):
        pass_on(q)
    block = feats.at[sib]
    remote(block, block, near_sem.at[0], near_sem.at[1], me_s, sib).wait_recv()
    acc[...] += dot(dense[sib], feats[sib])
    for d in range(1, ny):
        src = y_from(d)
        acc[...] += dot(dense[src], feats[src])
    for d in range(1, ny):
        src = ((y - d + ny) % ny) * 2 + 1 - core
        for q in range(CHUNKS):
            block = feats.at[src, pl.ds(q * step, step)]
            remote(block, block, f1_send.at[d, q], f1_recv.at[d, q], me_s, sib).wait_recv()
        acc[...] += dot(dense[src], feats[src])

    loads[1].wait()
    order = list(range(n // 2, n)) + list(range(1, n // 2))
    near = acc[...].astype(BF16)
    for h in range(HALVES):
        lanes = slice(h * cols, (h + 1) * cols)
        value = total[:, lanes] + dot(near, weights[1, :, lanes])
        hid[h] = jnp.maximum(value, 0.0).astype(BF16)
        for d in order:
            p = flip(me_s, d)
            r, c = piece(p)
            go(hid.at[h, r, c], by_time.at[h, me_s], p2_send.at[h, d], p2_recv.at[h, d], p, me_v)

    load_taps.wait()
    for h in range(HALVES):
        r, c = piece(me_s)
        by_time[h, me_s] = hid[h, r, c]
        for d in range(1, n):
            p = flip(me_s, d)
            block = by_time.at[h, p]
            remote(block, block, p2_send.at[h, d], p2_recv.at[h, d], p, me_v).wait_recv()
        shift = 0 if across == 1 else (me_s % across) * piece_cols
        for i in range(0, piece_rows, 16):
            for j in range(0, piece_cols, 128):
                at = h * cols + j + shift
                if across > 1:
                    at = pl.multiple_of(at, 128)
                filt = taps[:, pl.ds(at, 128)]
                wide = [by_time[h, t, i : i + 16, j : j + 128].astype(F32) for t in range(n)]
                for t in range(n):
                    value = filt[0:1] * wide[t]
                    for k in range(1, min(filt.shape[0] - 1, t) + 1):
                        value = value + filt[k : k + 1] * wide[t - k]
                    mix[h, t, i : i + 16, j : j + 128] = value.astype(BF16)
        for d in order:
            p = flip(me_s, d)
            go(mix.at[h, p], mixed.at[h, me_v, r, c], p3_send.at[h, d], p3_recv.at[h, d], p, me_v)
        mixed[h, me_v, r, c] = mix[h, me_s]

    half = rows // GROUPS
    size = n // GROUPS

    def group_rows(g):
        start = me_s // size if g == 0 else 1 - me_s // size
        return pl.ds(pl.multiple_of(start * half, half), half)

    def send_group(h, g):
        for d in range(g * size, (g + 1) * size):
            if d > 0:
                p = flip(me_s, d)
                r, c = piece(p)
                block = mixed.at[h, me_v, r, c]
                remote(block, block, p3_send.at[h, d], p3_recv.at[h, d], p, me_v).wait_recv()
        block = mixed.at[h, me_v, group_rows(g)]
        for d in range(1, ny):
            go(block, block, y4_send.at[d, h, g], y4_recv.at[d, h, g], me_s, y_to(d))
        go(block, block, s4_send.at[h, g], s4_recv.at[h, g], me_s, sib)

    def pass_group(h, g):
        for d in range(1, ny):
            src = y_from(d)
            block = mixed.at[h, src, group_rows(g)]
            remote(block, block, y4_send.at[d, h, g], y4_recv.at[d, h, g], me_s, src).wait_recv()
            go(block, block, f4_send.at[d, h, g], f4_recv.at[d, h, g], me_s, sib)

    def near_part(h):
        lanes = slice(h * cols, (h + 1) * cols)
        acc[:, lanes] = dot(dense[me_v], mixed[h, me_v])
        for g in range(GROUPS):
            block = mixed.at[h, sib, group_rows(g)]
            remote(block, block, s4_send.at[h, g], s4_recv.at[h, g], me_s, sib).wait_recv()
        acc[:, lanes] += dot(dense[sib], mixed[h, sib])
        own = dot(mixed[h, me_v], weights[2, lanes, :])
        if h == 0:
            total[...] = own
        else:
            total[...] += own

    def far_part(h):
        lanes = slice(h * cols, (h + 1) * cols)
        for d in range(1, ny):
            src = y_from(d)
            acc[:, lanes] += dot(dense[src], mixed[h, src])
        for d in range(1, ny):
            src = ((y - d + ny) % ny) * 2 + 1 - core
            for g in range(GROUPS):
                block = mixed.at[h, src, group_rows(g)]
                remote(block, block, f4_send.at[d, h, g], f4_recv.at[d, h, g], me_s, sib).wait_recv()
            acc[:, lanes] += dot(dense[src], mixed[h, src])
        total[...] += dot(acc[:, lanes].astype(BF16), weights[3, lanes, :])

    loads[2].wait()
    loads[3].wait()
    send_group(0, 0)
    send_group(0, 1)
    pass_group(0, 0)
    send_group(1, 0)
    pass_group(0, 1)
    near_part(0)
    send_group(1, 1)
    pass_group(1, 0)
    far_part(0)
    pass_group(1, 1)
    near_part(1)
    far_part(1)
    out[0] = jnp.maximum(total[...], 0.0).astype(BF16)
    for copy in sent:
        copy.wait_send()


def shards(n, nv, features, tile_values, tile_column, tile_count, *rest):
    _, rows, width = features.shape
    _, per, slots, tile, _ = tile_values.shape
    ny = nv // 2
    cols = width // HALVES
    piece_rows = max(rows // n, 16)
    piece_cols = cols // (n // (rows // piece_rows))
    taps = rest[2].shape[0]
    dma = pltpu.SemaphoreType.DMA
    hbm = pl.BlockSpec(memory_space=pltpu.HBM)
    return pl.pallas_call(
        functools.partial(kernel, (n, nv, rows, width, slots, tile)),
        out_shape=jax.ShapeDtypeStruct((1, rows, width), BF16),
        in_specs=[hbm] * 9,
        out_specs=pl.BlockSpec(memory_space=pltpu.VMEM),
        scratch_shapes=[
            pltpu.SMEM((per, slots), jnp.int32),
            pltpu.SMEM((1, per), jnp.int32),
            pltpu.VMEM((nv, rows, width), BF16),
            pltpu.VMEM((per, slots, tile, tile), BF16),
            pltpu.VMEM((nv, rows, rows), BF16),
            pltpu.VMEM((4, width, width), BF16),
            pltpu.VMEM((taps, width), F32),
            pltpu.VMEM((rows, width), F32),
            pltpu.VMEM((rows, width), F32),
            pltpu.VMEM((HALVES, rows, cols), BF16),
            pltpu.VMEM((HALVES, n, piece_rows, piece_cols), BF16),
            pltpu.VMEM((HALVES, n, piece_rows, piece_cols), BF16),
            pltpu.VMEM((HALVES, nv, rows, cols), BF16),
            dma((9,)),
            dma((2,)),
            dma((ny, CHUNKS)),
            dma((ny, CHUNKS)),
            dma((ny, CHUNKS)),
            dma((ny, CHUNKS)),
            dma((HALVES, n)),
            dma((HALVES, n)),
            dma((HALVES, n)),
            dma((HALVES, n)),
            dma((ny, HALVES, GROUPS)),
            dma((ny, HALVES, GROUPS)),
            dma((HALVES, GROUPS)),
            dma((HALVES, GROUPS)),
            dma((ny, HALVES, GROUPS)),
            dma((ny, HALVES, GROUPS)),
        ],
        compiler_params=pltpu.CompilerParams(
            collective_id=0, has_side_effects=True, vmem_limit_bytes=64 * 1024 * 1024
        ),
    )(features, tile_values, tile_column, tile_count, *rest)


def solution(mesh):
    n, nv = mesh.shape["snap"], mesh.shape["vert"]
    return jax.shard_map(
        functools.partial(shards, n, nv),
        mesh=mesh,
        in_specs=(
            P("snap", "vert", None),
            P("snap", "vert", None, None, None),
            P("snap", "vert", None),
            P("snap", "vert"),
            P(),
            P(),
            P(),
            P(),
            P(),
        ),
        out_specs=P("snap", "vert", None),
        check_vma=False,
    )
```

```python
import functools

import jax
import jax.numpy as jnp
from jax import lax
from jax.experimental import pallas as pl
from jax.experimental.pallas import tpu as pltpu
from jax.sharding import PartitionSpec as P

MESH = pl.DeviceIdType.MESH
GROUPS = 2
MOST_PARTS = 4
F32 = jnp.float32
BF16 = jnp.bfloat16


def cut(n, rows, width):
    piece_rows = max(rows // n, 16)
    across = n // (rows // piece_rows)
    parts = max(1, min(MOST_PARTS, width // 128 // across))
    return parts, width // parts, across, piece_rows, width // parts // across


def flip(index, mask):
    out, bit = index, 1
    while bit <= mask:
        if mask & bit:
            out = out + (1 - 2 * ((index // bit) % 2)) * bit
        bit *= 2
    return out


def kernel(
    sizes,
    features,
    tile_values,
    columns,
    counts,
    message_one,
    root_one,
    time_taps,
    message_two,
    root_two,
    out,
    column_smem,
    count_smem,
    feats,
    msgs,
    tiles,
    dense,
    weights,
    taps,
    acc,
    total,
    hid,
    by_time,
    mix,
    mixed,
    local_sem,
    near_send,
    near_recv,
    y1_send,
    y1_recv,
    f1_send,
    f1_recv,
    p2_send,
    p2_recv,
    p3_send,
    p3_recv,
    y4_send,
    y4_recv,
    s4_send,
    s4_recv,
    f4_send,
    f4_recv,
):
    n, nv, rows, width, slots, tile = sizes
    ny = nv // 2
    per = rows // tile
    parts, cols, across, piece_rows, piece_cols = cut(n, rows, width)
    me_s, me_v = lax.axis_index("snap"), lax.axis_index("vert")
    y, core = me_v // 2, me_v % 2
    sib = y * 2 + 1 - core

    def piece(p):
        r = pl.multiple_of((p // across) * piece_rows, piece_rows)
        if across == 1:
            return pl.ds(r, piece_rows), slice(0, piece_cols)
        return pl.ds(r, piece_rows), pl.ds(pl.multiple_of((p % across) * piece_cols, piece_cols), piece_cols)

    def remote(src, dst, send, recv, s, v):
        return pltpu.make_async_remote_copy(
            src_ref=src, dst_ref=dst, send_sem=send, recv_sem=recv, device_id=(s, v), device_id_type=MESH
        )

    sent = []

    def go(*args):
        copy = remote(*args)
        copy.start()
        sent.append(copy)

    def y_to(d):
        return ((y + d) % ny) * 2 + core

    def y_from(d):
        return ((y - d + ny) % ny) * 2 + core

    load_feats = pltpu.make_async_copy(features.at[0], feats, local_sem.at[0])
    load_tiles = pltpu.make_async_copy(tile_values.at[0], tiles, local_sem.at[1])
    loads = [
        pltpu.make_async_copy(ref, weights.at[i], local_sem.at[2 + i])
        for i, ref in enumerate((root_one, message_one, root_two, message_two))
    ]
    load_taps = pltpu.make_async_copy(time_taps, taps, local_sem.at[6])
    load_columns = pltpu.make_async_copy(columns.at[0], column_smem, local_sem.at[7])
    load_counts = pltpu.make_async_copy(counts, count_smem, local_sem.at[8])
    for load in (load_feats, loads[1], load_columns, load_counts, load_tiles, loads[0], load_taps, loads[2], loads[3]):
        load.start()

    barrier = pltpu.get_barrier_semaphore()
    for d in range(1, n):
        pl.semaphore_signal(barrier, inc=1, device_id=(flip(me_s, d), me_v), device_id_type=MESH)
    for d in range(1, ny):
        pl.semaphore_signal(barrier, inc=1, device_id=(me_s, y_to(d)), device_id_type=MESH)
    pl.semaphore_signal(barrier, inc=1, device_id=(me_s, sib), device_id_type=MESH)

    def dot(a, b):
        return jnp.dot(a, b, preferred_element_type=F32)

    def lanes(h):
        return slice(h * cols, (h + 1) * cols)

    load_feats.wait()
    loads[1].wait()
    for h in range(parts):
        msgs[h, me_v] = dot(feats[...], weights[1, :, lanes(h)]).astype(BF16)
        if h == 0:
            pl.semaphore_wait(barrier, n - 1 + ny)
        block = msgs.at[h, me_v]
        for d in range(1, ny):
            go(block, block, y1_send.at[d, h], y1_recv.at[d, h], me_s, y_to(d))
        go(block, block, near_send.at[h], near_recv.at[h], me_s, sib)

    def pass_on(h):
        for d in range(1, ny):
            src = y_from(d)
            block = msgs.at[h, src]
            remote(block, block, y1_send.at[d, h], y1_recv.at[d, h], me_s, src).wait_recv()
            go(block, block, f1_send.at[d, h], f1_recv.at[d, h], me_s, sib)

    load_columns.wait()
    load_counts.wait()
    load_tiles.wait()
    live = [
        [jnp.where(k < count_smem[0, b], column_smem[b, k], -1) for k in range(slots)] for b in range(per)
    ]

    def fill(v, carry):
        for b in range(per):
            for j in range(per):
                block = jnp.zeros((tile, tile), F32)
                for k in range(slots):
                    scale = jnp.where(live[b][k] == v * per + j, 1.0, 0.0).astype(F32)
                    block = block + scale * tiles[b, k].astype(F32)
                dense[v, b * tile : (b + 1) * tile, j * tile : (j + 1) * tile] = block.astype(BF16)
        return carry

    lax.fori_loop(0, nv, fill, 0)

    order = list(range(n // 2, n)) + list(range(1, n // 2))
    loads[0].wait()

    def near_messages(h):
        total[:, lanes(h)] = dot(feats[...], weights[0, :, lanes(h)])
        block = msgs.at[h, sib]
        remote(block, block, near_send.at[h], near_recv.at[h], me_s, sib).wait_recv()
        total[:, lanes(h)] += dot(dense[me_v], msgs[h, me_v]) + dot(dense[sib], msgs[h, sib])

    def far_messages(h):
        value = total[:, lanes(h)]
        for d in range(1, ny):
            src = y_from(d)
            value = value + dot(dense[src], msgs[h, src])
        for d in range(1, ny):
            src = ((y - d + ny) % ny) * 2 + 1 - core
            block = msgs.at[h, src]
            remote(block, block, f1_send.at[d, h], f1_recv.at[d, h], me_s, sib).wait_recv()
            value = value + dot(dense[src], msgs[h, src])
        hid[h] = jnp.maximum(value, 0.0).astype(BF16)
        for d in order:
            p = flip(me_s, d)
            r, c = piece(p)
            go(hid.at[h, r, c], by_time.at[h, me_s], p2_send.at[h, d], p2_recv.at[h, d], p, me_v)

    def filter_part(h):
        r, c = piece(me_s)
        by_time[h, me_s] = hid[h, r, c]
        for d in range(1, n):
            p = flip(me_s, d)
            block = by_time.at[h, p]
            remote(block, block, p2_send.at[h, d], p2_recv.at[h, d], p, me_v).wait_recv()
        shift = 0 if across == 1 else (me_s % across) * piece_cols
        for i in range(0, piece_rows, 16):
            for j in range(0, piece_cols, 128):
                at = h * cols + j + shift
                if across > 1:
                    at = pl.multiple_of(at, 128)
                filt = taps[:, pl.ds(at, 128)]
                wide = [by_time[h, t, i : i + 16, j : j + 128].astype(F32) for t in range(n)]
                for t in range(n):
                    value = filt[0:1] * wide[t]
                    for k in range(1, min(filt.shape[0] - 1, t) + 1):
                        value = value + filt[k : k + 1] * wide[t - k]
                    mix[h, t, i : i + 16, j : j + 128] = value.astype(BF16)
        for d in order:
            p = flip(me_s, d)
            go(mix.at[h, p], mixed.at[h, me_v, r, c], p3_send.at[h, d], p3_recv.at[h, d], p, me_v)
        mixed[h, me_v, r, c] = mix[h, me_s]

    pass_on(0)
    near_messages(0)
    load_taps.wait()
    for h in range(parts):
        if h + 1 < parts:
            pass_on(h + 1)
        far_messages(h)
        if h + 1 < parts:
            near_messages(h + 1)
        if h >= 2:
            filter_part(h - 2)
    for h in range(max(0, parts - 2), parts):
        filter_part(h)

    half = rows // GROUPS
    size = n // GROUPS

    def group_rows(g):
        start = me_s // size if g == 0 else 1 - me_s // size
        return pl.ds(pl.multiple_of(start * half, half), half)

    def send_group(h, g):
        for d in range(g * size, (g + 1) * size):
            if d > 0:
                p = flip(me_s, d)
                r, c = piece(p)
                block = mixed.at[h, me_v, r, c]
                remote(block, block, p3_send.at[h, d], p3_recv.at[h, d], p, me_v).wait_recv()
        block = mixed.at[h, me_v, group_rows(g)]
        for d in range(1, ny):
            go(block, block, y4_send.at[d, h, g], y4_recv.at[d, h, g], me_s, y_to(d))
        go(block, block, s4_send.at[h, g], s4_recv.at[h, g], me_s, sib)

    def pass_group(h, g):
        for d in range(1, ny):
            src = y_from(d)
            block = mixed.at[h, src, group_rows(g)]
            remote(block, block, y4_send.at[d, h, g], y4_recv.at[d, h, g], me_s, src).wait_recv()
            go(block, block, f4_send.at[d, h, g], f4_recv.at[d, h, g], me_s, sib)

    def near_part(h):
        value = dot(dense[me_v], mixed[h, me_v])
        for g in range(GROUPS):
            block = mixed.at[h, sib, group_rows(g)]
            remote(block, block, s4_send.at[h, g], s4_recv.at[h, g], me_s, sib).wait_recv()
        acc[:, lanes(h)] = value + dot(dense[sib], mixed[h, sib])
        own = dot(mixed[h, me_v], weights[2, lanes(h), :])
        if h == 0:
            total[...] = own
        else:
            total[...] += own

    def far_part(h):
        value = acc[:, lanes(h)]
        for d in range(1, ny):
            src = y_from(d)
            value = value + dot(dense[src], mixed[h, src])
        for d in range(1, ny):
            src = ((y - d + ny) % ny) * 2 + 1 - core
            for g in range(GROUPS):
                block = mixed.at[h, src, group_rows(g)]
                remote(block, block, f4_send.at[d, h, g], f4_recv.at[d, h, g], me_s, sib).wait_recv()
            value = value + dot(dense[src], mixed[h, src])
        last = dot(value.astype(BF16), weights[3, lanes(h), :])
        if h + 1 < parts:
            total[...] += last
        else:
            out[0] = (total[...] + last).astype(BF16)

    loads[2].wait()
    loads[3].wait()
    send_group(0, 0)
    send_group(0, 1)
    for h in range(parts):
        pass_group(h, 0)
        if h + 1 < parts:
            send_group(h + 1, 0)
        pass_group(h, 1)
        near_part(h)
        if h + 1 < parts:
            send_group(h + 1, 1)
        far_part(h)
    for copy in sent:
        copy.wait_send()


def shards(n, nv, features, tile_values, tile_column, tile_count, *rest):
    _, rows, width = features.shape
    _, per, slots, tile, _ = tile_values.shape
    ny = nv // 2
    parts, cols, _, piece_rows, piece_cols = cut(n, rows, width)
    taps = rest[2].shape[0]
    dma = pltpu.SemaphoreType.DMA
    hbm = pl.BlockSpec(memory_space=pltpu.HBM)
    summed = pl.pallas_call(
        functools.partial(kernel, (n, nv, rows, width, slots, tile)),
        out_shape=jax.ShapeDtypeStruct((1, rows, width), BF16),
        in_specs=[hbm] * 9,
        out_specs=pl.BlockSpec(memory_space=pltpu.VMEM),
        scratch_shapes=[
            pltpu.SMEM((per, slots), jnp.int32),
            pltpu.SMEM((1, per), jnp.int32),
            pltpu.VMEM((rows, width), BF16),
            pltpu.VMEM((parts, nv, rows, cols), BF16),
            pltpu.VMEM((per, slots, tile, tile), BF16),
            pltpu.VMEM((nv, rows, rows), BF16),
            pltpu.VMEM((4, width, width), BF16),
            pltpu.VMEM((taps, width), F32),
            pltpu.VMEM((rows, width), F32),
            pltpu.VMEM((rows, width), F32),
            pltpu.VMEM((parts, rows, cols), BF16),
            pltpu.VMEM((parts, n, piece_rows, piece_cols), BF16),
            pltpu.VMEM((parts, n, piece_rows, piece_cols), BF16),
            pltpu.VMEM((parts, nv, rows, cols), BF16),
            dma((9,)),
            dma((parts,)),
            dma((parts,)),
            dma((ny, parts)),
            dma((ny, parts)),
            dma((ny, parts)),
            dma((ny, parts)),
            dma((parts, n)),
            dma((parts, n)),
            dma((parts, n)),
            dma((parts, n)),
            dma((ny, parts, GROUPS)),
            dma((ny, parts, GROUPS)),
            dma((parts, GROUPS)),
            dma((parts, GROUPS)),
            dma((ny, parts, GROUPS)),
            dma((ny, parts, GROUPS)),
        ],
        compiler_params=pltpu.CompilerParams(
            collective_id=0, has_side_effects=True, vmem_limit_bytes=64 * 1024 * 1024
        ),
    )(features, tile_values, tile_column, tile_count, *rest)
    return jnp.maximum(summed, 0)


def solution(mesh):
    n, nv = mesh.shape["snap"], mesh.shape["vert"]
    return jax.shard_map(
        functools.partial(shards, n, nv),
        mesh=mesh,
        in_specs=(
            P("snap", "vert", None),
            P("snap", "vert", None, None, None),
            P("snap", "vert", None),
            P("snap", "vert"),
            P(),
            P(),
            P(),
            P(),
            P(),
        ),
        out_specs=P("snap", "vert", None),
        check_vma=False,
    )
```

```python
import functools

import jax
import jax.numpy as jnp
from jax import lax
from jax.experimental import pallas as pl
from jax.experimental.pallas import tpu as pltpu
from jax.sharding import PartitionSpec as P

MESH = pl.DeviceIdType.MESH
GROUPS = 2
MOST_PARTS = 2
F32 = jnp.float32
BF16 = jnp.bfloat16


def cut(n, rows, width):
    piece_rows = max(rows // n, 16)
    across = n // (rows // piece_rows)
    parts = max(1, min(MOST_PARTS, width // 128 // across))
    return parts, width // parts, across, piece_rows, width // parts // across


def flip(index, mask):
    out, bit = index, 1
    while bit <= mask:
        if mask & bit:
            out = out + (1 - 2 * ((index // bit) % 2)) * bit
        bit *= 2
    return out


def kernel(
    sizes,
    features,
    tile_values,
    columns,
    counts,
    message_one,
    root_one,
    time_taps,
    message_two,
    root_two,
    out,
    column_smem,
    count_smem,
    feats,
    msgs,
    tiles,
    dense,
    weights,
    taps,
    acc,
    total,
    hid,
    by_time,
    mix,
    mixed,
    local_sem,
    near_send,
    near_recv,
    y1_send,
    y1_recv,
    f1_send,
    f1_recv,
    p2_send,
    p2_recv,
    p3_send,
    p3_recv,
    y4_send,
    y4_recv,
    s4_send,
    s4_recv,
    f4_send,
    f4_recv,
):
    n, nv, rows, width, slots, tile = sizes
    ny = nv // 2
    per = rows // tile
    parts, cols, across, piece_rows, piece_cols = cut(n, rows, width)
    me_s, me_v = lax.axis_index("snap"), lax.axis_index("vert")
    y, core = me_v // 2, me_v % 2
    sib = y * 2 + 1 - core

    def piece(p):
        r = pl.multiple_of((p // across) * piece_rows, piece_rows)
        if across == 1:
            return pl.ds(r, piece_rows), slice(0, piece_cols)
        return pl.ds(r, piece_rows), pl.ds(pl.multiple_of((p % across) * piece_cols, piece_cols), piece_cols)

    def remote(src, dst, send, recv, s, v):
        return pltpu.make_async_remote_copy(
            src_ref=src, dst_ref=dst, send_sem=send, recv_sem=recv, device_id=(s, v), device_id_type=MESH
        )

    sent = []

    def go(*args):
        copy = remote(*args)
        copy.start()
        sent.append(copy)

    def y_to(d):
        return ((y + d) % ny) * 2 + core

    def y_from(d):
        return ((y - d + ny) % ny) * 2 + core

    load_feats = pltpu.make_async_copy(features.at[0], feats, local_sem.at[0])
    load_tiles = pltpu.make_async_copy(tile_values.at[0], tiles, local_sem.at[1])
    loads = [
        pltpu.make_async_copy(ref, weights.at[i], local_sem.at[2 + i])
        for i, ref in enumerate((root_one, message_one, root_two, message_two))
    ]
    load_taps = pltpu.make_async_copy(time_taps, taps, local_sem.at[6])
    load_columns = pltpu.make_async_copy(columns.at[0], column_smem, local_sem.at[7])
    load_counts = pltpu.make_async_copy(counts, count_smem, local_sem.at[8])
    for load in (load_feats, loads[1], load_columns, load_counts, load_tiles, loads[0], load_taps, loads[2], loads[3]):
        load.start()

    barrier = pltpu.get_barrier_semaphore()
    for d in range(1, n):
        pl.semaphore_signal(barrier, inc=1, device_id=(flip(me_s, d), me_v), device_id_type=MESH)
    for d in range(1, ny):
        pl.semaphore_signal(barrier, inc=1, device_id=(me_s, y_to(d)), device_id_type=MESH)
    pl.semaphore_signal(barrier, inc=1, device_id=(me_s, sib), device_id_type=MESH)

    def dot(a, b):
        return jnp.dot(a, b, preferred_element_type=F32)

    def lanes(h):
        return slice(h * cols, (h + 1) * cols)

    load_feats.wait()
    loads[1].wait()
    for h in range(parts):
        msgs[h, me_v] = dot(feats[...], weights[1, :, lanes(h)]).astype(BF16)
        if h == 0:
            pl.semaphore_wait(barrier, n - 1 + ny)
        block = msgs.at[h, me_v]
        for d in range(1, ny):
            go(block, block, y1_send.at[d, h], y1_recv.at[d, h], me_s, y_to(d))
        go(block, block, near_send.at[h], near_recv.at[h], me_s, sib)

    def pass_on(h):
        for d in range(1, ny):
            src = y_from(d)
            block = msgs.at[h, src]
            remote(block, block, y1_send.at[d, h], y1_recv.at[d, h], me_s, src).wait_recv()
            go(block, block, f1_send.at[d, h], f1_recv.at[d, h], me_s, sib)

    load_columns.wait()
    load_counts.wait()
    load_tiles.wait()
    live = [
        [jnp.where(k < count_smem[0, b], column_smem[b, k], -1) for k in range(slots)] for b in range(per)
    ]

    def fill(v, carry):
        for b in range(per):
            for j in range(per):
                block = jnp.zeros((tile, tile), F32)
                for k in range(slots):
                    scale = jnp.where(live[b][k] == v * per + j, 1.0, 0.0).astype(F32)
                    block = block + scale * tiles[b, k].astype(F32)
                dense[v, b * tile : (b + 1) * tile, j * tile : (j + 1) * tile] = block.astype(BF16)
        return carry

    lax.fori_loop(0, nv, fill, 0)

    order = list(range(n // 2, n)) + list(range(1, n // 2))
    loads[0].wait()

    def near_messages(h):
        total[:, lanes(h)] = dot(feats[...], weights[0, :, lanes(h)])
        block = msgs.at[h, sib]
        remote(block, block, near_send.at[h], near_recv.at[h], me_s, sib).wait_recv()
        total[:, lanes(h)] += dot(dense[me_v], msgs[h, me_v]) + dot(dense[sib], msgs[h, sib])

    def far_messages(h):
        value = total[:, lanes(h)]
        for d in range(1, ny):
            src = y_from(d)
            value = value + dot(dense[src], msgs[h, src])
        for d in range(1, ny):
            src = ((y - d + ny) % ny) * 2 + 1 - core
            block = msgs.at[h, src]
            remote(block, block, f1_send.at[d, h], f1_recv.at[d, h], me_s, sib).wait_recv()
            value = value + dot(dense[src], msgs[h, src])
        hid[h] = jnp.maximum(value, 0.0).astype(BF16)
        for d in order:
            p = flip(me_s, d)
            r, c = piece(p)
            go(hid.at[h, r, c], by_time.at[h, me_s], p2_send.at[h, d], p2_recv.at[h, d], p, me_v)

    def filter_part(h):
        r, c = piece(me_s)
        by_time[h, me_s] = hid[h, r, c]
        for d in range(1, n):
            p = flip(me_s, d)
            block = by_time.at[h, p]
            remote(block, block, p2_send.at[h, d], p2_recv.at[h, d], p, me_v).wait_recv()
        shift = 0 if across == 1 else (me_s % across) * piece_cols
        for i in range(0, piece_rows, 16):
            for j in range(0, piece_cols, 128):
                at = h * cols + j + shift
                if across > 1:
                    at = pl.multiple_of(at, 128)
                filt = taps[:, pl.ds(at, 128)]
                wide = [by_time[h, t, i : i + 16, j : j + 128].astype(F32) for t in range(n)]
                for t in range(n):
                    value = filt[0:1] * wide[t]
                    for k in range(1, min(filt.shape[0] - 1, t) + 1):
                        value = value + filt[k : k + 1] * wide[t - k]
                    mix[h, t, i : i + 16, j : j + 128] = value.astype(BF16)
        for d in order:
            p = flip(me_s, d)
            go(mix.at[h, p], mixed.at[h, me_v, r, c], p3_send.at[h, d], p3_recv.at[h, d], p, me_v)
        mixed[h, me_v, r, c] = mix[h, me_s]

    pass_on(0)
    near_messages(0)
    load_taps.wait()
    for h in range(parts):
        if h + 1 < parts:
            pass_on(h + 1)
        far_messages(h)
        if h + 1 < parts:
            near_messages(h + 1)
        if h >= 2:
            filter_part(h - 2)
    for h in range(max(0, parts - 2), parts):
        filter_part(h)

    half = rows // GROUPS
    size = n // GROUPS

    def group_rows(g):
        start = me_s // size if g == 0 else 1 - me_s // size
        return pl.ds(pl.multiple_of(start * half, half), half)

    def send_group(h, g):
        for d in range(g * size, (g + 1) * size):
            if d > 0:
                p = flip(me_s, d)
                r, c = piece(p)
                block = mixed.at[h, me_v, r, c]
                remote(block, block, p3_send.at[h, d], p3_recv.at[h, d], p, me_v).wait_recv()
        block = mixed.at[h, me_v, group_rows(g)]
        for d in range(1, ny):
            go(block, block, y4_send.at[d, h, g], y4_recv.at[d, h, g], me_s, y_to(d))
        go(block, block, s4_send.at[h, g], s4_recv.at[h, g], me_s, sib)

    def pass_group(h, g):
        for d in range(1, ny):
            src = y_from(d)
            block = mixed.at[h, src, group_rows(g)]
            remote(block, block, y4_send.at[d, h, g], y4_recv.at[d, h, g], me_s, src).wait_recv()
            go(block, block, f4_send.at[d, h, g], f4_recv.at[d, h, g], me_s, sib)

    def near_part(h):
        value = dot(dense[me_v], mixed[h, me_v])
        for g in range(GROUPS):
            block = mixed.at[h, sib, group_rows(g)]
            remote(block, block, s4_send.at[h, g], s4_recv.at[h, g], me_s, sib).wait_recv()
        acc[:, lanes(h)] = value + dot(dense[sib], mixed[h, sib])
        own = dot(mixed[h, me_v], weights[2, lanes(h), :])
        if h == 0:
            total[...] = own
        else:
            total[...] += own

    def far_part(h):
        value = acc[:, lanes(h)]
        for d in range(1, ny):
            src = y_from(d)
            value = value + dot(dense[src], mixed[h, src])
        for d in range(1, ny):
            src = ((y - d + ny) % ny) * 2 + 1 - core
            for g in range(GROUPS):
                block = mixed.at[h, src, group_rows(g)]
                remote(block, block, f4_send.at[d, h, g], f4_recv.at[d, h, g], me_s, sib).wait_recv()
            value = value + dot(dense[src], mixed[h, src])
        last = dot(value.astype(BF16), weights[3, lanes(h), :])
        if h + 1 < parts:
            total[...] += last
        else:
            out[0] = (total[...] + last).astype(BF16)

    loads[2].wait()
    loads[3].wait()
    send_group(0, 0)
    send_group(0, 1)
    for h in range(parts):
        pass_group(h, 0)
        if h + 1 < parts:
            send_group(h + 1, 0)
        pass_group(h, 1)
        near_part(h)
        if h + 1 < parts:
            send_group(h + 1, 1)
        far_part(h)
    for copy in sent:
        copy.wait_send()


def shards(n, nv, features, tile_values, tile_column, tile_count, *rest):
    _, rows, width = features.shape
    _, per, slots, tile, _ = tile_values.shape
    ny = nv // 2
    parts, cols, _, piece_rows, piece_cols = cut(n, rows, width)
    taps = rest[2].shape[0]
    dma = pltpu.SemaphoreType.DMA
    hbm = pl.BlockSpec(memory_space=pltpu.HBM)
    summed = pl.pallas_call(
        functools.partial(kernel, (n, nv, rows, width, slots, tile)),
        out_shape=jax.ShapeDtypeStruct((1, rows, width), BF16),
        in_specs=[hbm] * 9,
        out_specs=pl.BlockSpec(memory_space=pltpu.VMEM),
        scratch_shapes=[
            pltpu.SMEM((per, slots), jnp.int32),
            pltpu.SMEM((1, per), jnp.int32),
            pltpu.VMEM((rows, width), BF16),
            pltpu.VMEM((parts, nv, rows, cols), BF16),
            pltpu.VMEM((per, slots, tile, tile), BF16),
            pltpu.VMEM((nv, rows, rows), BF16),
            pltpu.VMEM((4, width, width), BF16),
            pltpu.VMEM((taps, width), F32),
            pltpu.VMEM((rows, width), F32),
            pltpu.VMEM((rows, width), F32),
            pltpu.VMEM((parts, rows, cols), BF16),
            pltpu.VMEM((parts, n, piece_rows, piece_cols), BF16),
            pltpu.VMEM((parts, n, piece_rows, piece_cols), BF16),
            pltpu.VMEM((parts, nv, rows, cols), BF16),
            dma((9,)),
            dma((parts,)),
            dma((parts,)),
            dma((ny, parts)),
            dma((ny, parts)),
            dma((ny, parts)),
            dma((ny, parts)),
            dma((parts, n)),
            dma((parts, n)),
            dma((parts, n)),
            dma((parts, n)),
            dma((ny, parts, GROUPS)),
            dma((ny, parts, GROUPS)),
            dma((parts, GROUPS)),
            dma((parts, GROUPS)),
            dma((ny, parts, GROUPS)),
            dma((ny, parts, GROUPS)),
        ],
        compiler_params=pltpu.CompilerParams(
            collective_id=0, has_side_effects=True, vmem_limit_bytes=64 * 1024 * 1024
        ),
    )(features, tile_values, tile_column, tile_count, *rest)
    return jnp.maximum(summed, 0)


def solution(mesh):
    n, nv = mesh.shape["snap"], mesh.shape["vert"]
    return jax.shard_map(
        functools.partial(shards, n, nv),
        mesh=mesh,
        in_specs=(
            P("snap", "vert", None),
            P("snap", "vert", None, None, None),
            P("snap", "vert", None),
            P("snap", "vert"),
            P(),
            P(),
            P(),
            P(),
            P(),
        ),
        out_specs=P("snap", "vert", None),
        check_vma=False,
    )
```

```python
import functools

import jax
import jax.numpy as jnp
from jax import lax
from jax.experimental import pallas as pl
from jax.experimental.pallas import tpu as pltpu
from jax.sharding import PartitionSpec as P

MESH = pl.DeviceIdType.MESH
GROUPS = 2
MOST_PARTS = 2
F32 = jnp.float32
BF16 = jnp.bfloat16


def cut(n, rows, width):
    piece_rows = max(rows // n, 16)
    across = n // (rows // piece_rows)
    parts = max(1, min(MOST_PARTS, width // 128 // across))
    return parts, width // parts, across, piece_rows, width // parts // across


def flip(index, mask):
    out, bit = index, 1
    while bit <= mask:
        if mask & bit:
            out = out + (1 - 2 * ((index // bit) % 2)) * bit
        bit *= 2
    return out


def kernel(
    sizes,
    features,
    tile_values,
    columns,
    counts,
    message_one,
    root_one,
    time_taps,
    message_two,
    root_two,
    out,
    column_smem,
    count_smem,
    feats,
    msgs,
    tiles,
    dense,
    weights,
    taps,
    acc,
    total,
    hid,
    by_time,
    mix,
    mixed,
    local_sem,
    near_send,
    near_recv,
    y1_send,
    y1_recv,
    f1_send,
    f1_recv,
    p2_send,
    p2_recv,
    p3_send,
    p3_recv,
    y4_send,
    y4_recv,
    s4_send,
    s4_recv,
    f4_send,
    f4_recv,
):
    n, nv, rows, width, slots, tile = sizes
    ny = nv // 2
    per = rows // tile
    parts, cols, across, piece_rows, piece_cols = cut(n, rows, width)
    me_s, me_v = lax.axis_index("snap"), lax.axis_index("vert")
    y, core = me_v // 2, me_v % 2
    sib = y * 2 + 1 - core

    def piece(p):
        r = pl.multiple_of((p // across) * piece_rows, piece_rows)
        if across == 1:
            return pl.ds(r, piece_rows), slice(0, piece_cols)
        return pl.ds(r, piece_rows), pl.ds(pl.multiple_of((p % across) * piece_cols, piece_cols), piece_cols)

    def remote(src, dst, send, recv, s, v):
        return pltpu.make_async_remote_copy(
            src_ref=src, dst_ref=dst, send_sem=send, recv_sem=recv, device_id=(s, v), device_id_type=MESH
        )

    sent = []

    def go(*args):
        copy = remote(*args)
        copy.start()
        sent.append(copy)

    def pieces_arrived(h, count, recv):
        block = by_time.at[h, pl.ds(0, count)]
        remote(block, block, recv, recv, me_s, sib).wait_recv()

    def pieces_left(h, send):
        block = by_time.at[h, pl.ds(0, n - 1)]
        remote(block, block, send, send, me_s, sib).wait_send()

    def all_left():
        for copy in sent:
            copy.wait_send()
        sent.clear()

    def y_to(d):
        return ((y + d) % ny) * 2 + core

    def y_from(d):
        return ((y - d + ny) % ny) * 2 + core

    load_feats = pltpu.make_async_copy(features.at[0], feats, local_sem.at[0])
    load_tiles = pltpu.make_async_copy(tile_values.at[0], tiles, local_sem.at[1])
    loads = [
        pltpu.make_async_copy(ref, weights.at[i], local_sem.at[2 + i])
        for i, ref in enumerate((root_one, message_one, root_two, message_two))
    ]
    load_taps = pltpu.make_async_copy(time_taps, taps, local_sem.at[6])
    load_columns = pltpu.make_async_copy(columns.at[0], column_smem, local_sem.at[7])
    load_counts = pltpu.make_async_copy(counts, count_smem, local_sem.at[8])
    for load in (load_feats, loads[1], load_columns, load_counts, load_tiles, loads[0], load_taps, loads[2], loads[3]):
        load.start()

    barrier = pltpu.get_barrier_semaphore()
    for d in range(1, n):
        pl.semaphore_signal(barrier, inc=1, device_id=(flip(me_s, d), me_v), device_id_type=MESH)
    for d in range(1, ny):
        pl.semaphore_signal(barrier, inc=1, device_id=(me_s, y_to(d)), device_id_type=MESH)
    pl.semaphore_signal(barrier, inc=1, device_id=(me_s, sib), device_id_type=MESH)

    def dot(a, b):
        return jnp.dot(a, b, preferred_element_type=F32)

    def lanes(h):
        return slice(h * cols, (h + 1) * cols)

    load_feats.wait()
    loads[1].wait()
    for h in range(parts):
        msgs[h, me_v] = dot(feats[...], weights[1, :, lanes(h)]).astype(BF16)
        if h == 0:
            pl.semaphore_wait(barrier, n - 1 + ny)
        block = msgs.at[h, me_v]
        for d in range(1, ny):
            go(block, block, y1_send.at[d, h], y1_recv.at[d, h], me_s, y_to(d))
        go(block, block, near_send.at[h], near_recv.at[h], me_s, sib)

    def pass_on(h):
        for d in range(1, ny):
            src = y_from(d)
            block = msgs.at[h, src]
            remote(block, block, y1_send.at[d, h], y1_recv.at[d, h], me_s, src).wait_recv()
            go(block, block, f1_send.at[d, h], f1_recv.at[d, h], me_s, sib)

    load_columns.wait()
    load_counts.wait()
    load_tiles.wait()
    live = [
        [jnp.where(k < count_smem[0, b], column_smem[b, k], -1) for k in range(slots)] for b in range(per)
    ]

    def fill(v, carry):
        for b in range(per):
            for j in range(per):
                block = jnp.zeros((tile, tile), F32)
                for k in range(slots):
                    scale = jnp.where(live[b][k] == v * per + j, 1.0, 0.0).astype(F32)
                    block = block + scale * tiles[b, k].astype(F32)
                dense[v, b * tile : (b + 1) * tile, j * tile : (j + 1) * tile] = block.astype(BF16)
        return carry

    lax.fori_loop(0, nv, fill, 0)

    order = list(range(n // 2, n)) + list(range(1, n // 2))
    loads[0].wait()

    def near_messages(h):
        total[:, lanes(h)] = dot(feats[...], weights[0, :, lanes(h)])
        block = msgs.at[h, sib]
        remote(block, block, near_send.at[h], near_recv.at[h], me_s, sib).wait_recv()
        total[:, lanes(h)] += dot(dense[me_v], msgs[h, me_v]) + dot(dense[sib], msgs[h, sib])

    def far_messages(h):
        value = total[:, lanes(h)]
        for d in range(1, ny):
            src = y_from(d)
            value = value + dot(dense[src], msgs[h, src])
        for d in range(1, ny):
            src = ((y - d + ny) % ny) * 2 + 1 - core
            block = msgs.at[h, src]
            remote(block, block, f1_send.at[d, h], f1_recv.at[d, h], me_s, sib).wait_recv()
            value = value + dot(dense[src], msgs[h, src])
        hid[h] = jnp.maximum(value, 0.0).astype(BF16)
        for d in order:
            p = flip(me_s, d)
            r, c = piece(p)
            remote(hid.at[h, r, c], by_time.at[h, me_s], p2_send.at[h], p2_recv.at[h], p, me_v).start()

    def filter_part(h):
        r, c = piece(me_s)
        by_time[h, me_s] = hid[h, r, c]
        pieces_arrived(h, n - 1, p2_recv.at[h])
        shift = 0 if across == 1 else (me_s % across) * piece_cols
        for i in range(0, piece_rows, 16):
            for j in range(0, piece_cols, 128):
                at = h * cols + j + shift
                if across > 1:
                    at = pl.multiple_of(at, 128)
                filt = taps[:, pl.ds(at, 128)]
                wide = [by_time[h, t, i : i + 16, j : j + 128].astype(F32) for t in range(n)]
                for t in range(n):
                    value = filt[0:1] * wide[t]
                    for k in range(1, min(filt.shape[0] - 1, t) + 1):
                        value = value + filt[k : k + 1] * wide[t - k]
                    mix[h, t, i : i + 16, j : j + 128] = value.astype(BF16)
        for d in order:
            p = flip(me_s, d)
            remote(
                mix.at[h, p], mixed.at[h, me_v, r, c], p3_send.at[h], p3_recv.at[h, d // (n // GROUPS)], p, me_v
            ).start()
        mixed[h, me_v, r, c] = mix[h, me_s]

    pass_on(0)
    near_messages(0)
    load_taps.wait()
    for h in range(parts):
        if h + 1 < parts:
            pass_on(h + 1)
        far_messages(h)
        if h + 1 < parts:
            near_messages(h + 1)
        if h >= 2:
            filter_part(h - 2)
    for h in range(max(0, parts - 2), parts):
        filter_part(h)

    half = rows // GROUPS
    size = n // GROUPS

    def group_rows(g):
        start = me_s // size if g == 0 else 1 - me_s // size
        return pl.ds(pl.multiple_of(start * half, half), half)

    def send_group(h, g):
        pieces_arrived(h, size if g else size - 1, p3_recv.at[h, g])
        block = mixed.at[h, me_v, group_rows(g)]
        for d in range(1, ny):
            go(block, block, y4_send.at[d, h, g], y4_recv.at[d, h, g], me_s, y_to(d))
        if g + 1 == GROUPS:
            block = mixed.at[h, me_v]
            go(block, block, s4_send.at[h], s4_recv.at[h], me_s, sib)

    def pass_group(h, g):
        for d in range(1, ny):
            src = y_from(d)
            block = mixed.at[h, src, group_rows(g)]
            remote(block, block, y4_send.at[d, h, g], y4_recv.at[d, h, g], me_s, src).wait_recv()
            go(block, block, f4_send.at[d, h, g], f4_recv.at[d, h, g], me_s, sib)

    def near_part(h):
        value = dot(dense[me_v], mixed[h, me_v])
        block = mixed.at[h, sib]
        remote(block, block, s4_send.at[h], s4_recv.at[h], me_s, sib).wait_recv()
        acc[:, lanes(h)] = value + dot(dense[sib], mixed[h, sib])
        own = dot(mixed[h, me_v], weights[2, lanes(h), :])
        if h == 0:
            total[...] = own
        else:
            total[...] += own

    def far_part(h):
        value = acc[:, lanes(h)]
        for d in range(1, ny):
            src = y_from(d)
            value = value + dot(dense[src], mixed[h, src])
        for d in range(1, ny):
            src = ((y - d + ny) % ny) * 2 + 1 - core
            for g in range(GROUPS):
                block = mixed.at[h, src, group_rows(g)]
                remote(block, block, f4_send.at[d, h, g], f4_recv.at[d, h, g], me_s, sib).wait_recv()
            value = value + dot(dense[src], mixed[h, src])
        last = dot(value.astype(BF16), weights[3, lanes(h), :])
        if h + 1 < parts:
            total[...] += last
        else:
            out[0] = (total[...] + last).astype(BF16)

    loads[2].wait()
    loads[3].wait()
    all_left()
    for h in range(parts):
        pieces_left(h, p2_send.at[h])
    send_group(0, 0)
    send_group(0, 1)
    for h in range(parts):
        pass_group(h, 0)
        if h + 1 < parts:
            send_group(h + 1, 0)
        pass_group(h, 1)
        near_part(h)
        if h + 1 < parts:
            send_group(h + 1, 1)
            pieces_left(h, p3_send.at[h])
        far_part(h)
    pieces_left(parts - 1, p3_send.at[parts - 1])
    all_left()


def shards(n, nv, features, tile_values, tile_column, tile_count, *rest):
    _, rows, width = features.shape
    _, per, slots, tile, _ = tile_values.shape
    ny = nv // 2
    parts, cols, _, piece_rows, piece_cols = cut(n, rows, width)
    taps = rest[2].shape[0]
    dma = pltpu.SemaphoreType.DMA
    hbm = pl.BlockSpec(memory_space=pltpu.HBM)
    summed = pl.pallas_call(
        functools.partial(kernel, (n, nv, rows, width, slots, tile)),
        out_shape=jax.ShapeDtypeStruct((1, rows, width), BF16),
        in_specs=[hbm] * 9,
        out_specs=pl.BlockSpec(memory_space=pltpu.VMEM),
        scratch_shapes=[
            pltpu.SMEM((per, slots), jnp.int32),
            pltpu.SMEM((1, per), jnp.int32),
            pltpu.VMEM((rows, width), BF16),
            pltpu.VMEM((parts, nv, rows, cols), BF16),
            pltpu.VMEM((per, slots, tile, tile), BF16),
            pltpu.VMEM((nv, rows, rows), BF16),
            pltpu.VMEM((4, width, width), BF16),
            pltpu.VMEM((taps, width), F32),
            pltpu.VMEM((rows, width), F32),
            pltpu.VMEM((rows, width), F32),
            pltpu.VMEM((parts, rows, cols), BF16),
            pltpu.VMEM((parts, n, piece_rows, piece_cols), BF16),
            pltpu.VMEM((parts, n, piece_rows, piece_cols), BF16),
            pltpu.VMEM((parts, nv, rows, cols), BF16),
            dma((9,)),
            dma((parts,)),
            dma((parts,)),
            dma((ny, parts)),
            dma((ny, parts)),
            dma((ny, parts)),
            dma((ny, parts)),
            dma((parts,)),
            dma((parts,)),
            dma((parts,)),
            dma((parts, GROUPS)),
            dma((ny, parts, GROUPS)),
            dma((ny, parts, GROUPS)),
            dma((parts,)),
            dma((parts,)),
            dma((ny, parts, GROUPS)),
            dma((ny, parts, GROUPS)),
        ],
        compiler_params=pltpu.CompilerParams(
            collective_id=0, has_side_effects=True, vmem_limit_bytes=64 * 1024 * 1024
        ),
    )(features, tile_values, tile_column, tile_count, *rest)
    return jnp.maximum(summed, 0)


def solution(mesh):
    n, nv = mesh.shape["snap"], mesh.shape["vert"]
    return jax.shard_map(
        functools.partial(shards, n, nv),
        mesh=mesh,
        in_specs=(
            P("snap", "vert", None),
            P("snap", "vert", None, None, None),
            P("snap", "vert", None),
            P("snap", "vert"),
            P(),
            P(),
            P(),
            P(),
            P(),
        ),
        out_specs=P("snap", "vert", None),
        check_vma=False,
    )
```

```python
import functools

import jax
import jax.numpy as jnp
from jax import lax
from jax.experimental import pallas as pl
from jax.experimental.pallas import tpu as pltpu
from jax.sharding import PartitionSpec as P

MESH = pl.DeviceIdType.MESH
GROUPS = 2
MOST_PARTS = 2
F32 = jnp.float32
BF16 = jnp.bfloat16


def cut(n, rows, width):
    piece_rows = max(rows // n, 16)
    across = n // (rows // piece_rows)
    parts = max(1, min(MOST_PARTS, width // 128 // across))
    return parts, width // parts, across, piece_rows, width // parts // across


def flip(index, mask):
    out, bit = index, 1
    while bit <= mask:
        if mask & bit:
            out = out + (1 - 2 * ((index // bit) % 2)) * bit
        bit *= 2
    return out


def kernel(
    sizes,
    features,
    tile_values,
    columns,
    counts,
    message_one,
    root_one,
    time_taps,
    message_two,
    root_two,
    out,
    column_smem,
    count_smem,
    feats,
    msgs,
    tiles,
    dense,
    weights,
    taps,
    acc,
    total,
    hid,
    by_time,
    mix,
    mixed,
    local_sem,
    near_send,
    near_recv,
    y1_send,
    y1_recv,
    f1_send,
    f1_recv,
    p2_send,
    p2_recv,
    p3_send,
    p3_recv,
    y4_send,
    y4_recv,
    s4_send,
    s4_recv,
    f4_send,
    f4_recv,
):
    n, nv, rows, width, slots, tile = sizes
    ny = nv // 2
    per = rows // tile
    parts, cols, across, piece_rows, piece_cols = cut(n, rows, width)
    me_s, me_v = lax.axis_index("snap"), lax.axis_index("vert")
    y, core = me_v // 2, me_v % 2
    sib = y * 2 + 1 - core

    def piece(p):
        r = pl.multiple_of((p // across) * piece_rows, piece_rows)
        if across == 1:
            return pl.ds(r, piece_rows), slice(0, piece_cols)
        return pl.ds(r, piece_rows), pl.ds(pl.multiple_of((p % across) * piece_cols, piece_cols), piece_cols)

    def remote(src, dst, send, recv, s, v):
        return pltpu.make_async_remote_copy(
            src_ref=src, dst_ref=dst, send_sem=send, recv_sem=recv, device_id=(s, v), device_id_type=MESH
        )

    sent = []

    def go(*args):
        copy = remote(*args)
        copy.start()
        sent.append(copy)

    def pieces_arrived(h, count, recv):
        block = by_time.at[h, pl.ds(0, count)]
        remote(block, block, recv, recv, me_s, sib).wait_recv()

    def pieces_left(h, send):
        block = by_time.at[h, pl.ds(0, n - 1)]
        remote(block, block, send, send, me_s, sib).wait_send()

    def all_left():
        for copy in sent:
            copy.wait_send()
        sent.clear()

    def y_to(d):
        return ((y + d) % ny) * 2 + core

    def y_from(d):
        return ((y - d + ny) % ny) * 2 + core

    load_feats = pltpu.make_async_copy(features.at[0], feats, local_sem.at[0])
    load_tiles = pltpu.make_async_copy(tile_values.at[0], tiles, local_sem.at[1])
    loads = [
        pltpu.make_async_copy(ref, weights.at[i], local_sem.at[2 + i])
        for i, ref in enumerate((root_one, message_one, root_two, message_two))
    ]
    load_taps = pltpu.make_async_copy(time_taps, taps, local_sem.at[6])
    load_columns = pltpu.make_async_copy(columns.at[0], column_smem, local_sem.at[7])
    load_counts = pltpu.make_async_copy(counts, count_smem, local_sem.at[8])
    load_feats.start()
    loads[1].start()
    barrier = pltpu.get_barrier_semaphore()
    for d in range(1, n):
        pl.semaphore_signal(barrier, inc=1, device_id=(flip(me_s, d), me_v), device_id_type=MESH)
    for d in range(1, ny):
        pl.semaphore_signal(barrier, inc=1, device_id=(me_s, y_to(d)), device_id_type=MESH)
    pl.semaphore_signal(barrier, inc=1, device_id=(me_s, sib), device_id_type=MESH)
    for load in (load_columns, load_counts, load_tiles, loads[0], load_taps, loads[2], loads[3]):
        load.start()

    def dot(a, b):
        return jnp.dot(a, b, preferred_element_type=F32)

    def lanes(h):
        return slice(h * cols, (h + 1) * cols)

    load_feats.wait()
    loads[1].wait()
    for h in range(parts):
        msgs[h, me_v] = dot(feats[...], weights[1, :, lanes(h)]).astype(BF16)
        if h == 0:
            pl.semaphore_wait(barrier, n - 1 + ny)
        block = msgs.at[h, me_v]
        for d in range(1, ny):
            go(block, block, y1_send.at[d, h], y1_recv.at[d, h], me_s, y_to(d))
        go(block, block, near_send.at[h], near_recv.at[h], me_s, sib)

    def pass_on(h):
        for d in range(1, ny):
            src = y_from(d)
            block = msgs.at[h, src]
            remote(block, block, y1_send.at[d, h], y1_recv.at[d, h], me_s, src).wait_recv()
            go(block, block, f1_send.at[d, h], f1_recv.at[d, h], me_s, sib)

    load_columns.wait()
    load_counts.wait()
    load_tiles.wait()
    live = [
        [jnp.where(k < count_smem[0, b], column_smem[b, k], -1) for k in range(slots)] for b in range(per)
    ]

    def fill(v, carry):
        for b in range(per):
            for j in range(per):
                block = jnp.zeros((tile, tile), F32)
                for k in range(slots):
                    scale = jnp.where(live[b][k] == v * per + j, 1.0, 0.0).astype(F32)
                    block = block + scale * tiles[b, k].astype(F32)
                dense[v, b * tile : (b + 1) * tile, j * tile : (j + 1) * tile] = block.astype(BF16)
        return carry

    lax.fori_loop(0, nv, fill, 0)

    order = list(range(n // 2, n)) + list(range(1, n // 2))
    loads[0].wait()

    def near_messages(h):
        total[:, lanes(h)] = dot(feats[...], weights[0, :, lanes(h)])
        block = msgs.at[h, sib]
        remote(block, block, near_send.at[h], near_recv.at[h], me_s, sib).wait_recv()
        total[:, lanes(h)] += dot(dense[me_v], msgs[h, me_v]) + dot(dense[sib], msgs[h, sib])

    def far_messages(h):
        value = total[:, lanes(h)]
        for d in range(1, ny):
            src = y_from(d)
            value = value + dot(dense[src], msgs[h, src])
        for d in range(1, ny):
            src = ((y - d + ny) % ny) * 2 + 1 - core
            block = msgs.at[h, src]
            remote(block, block, f1_send.at[d, h], f1_recv.at[d, h], me_s, sib).wait_recv()
            value = value + dot(dense[src], msgs[h, src])
        hid[h] = jnp.maximum(value, 0.0).astype(BF16)
        for d in order:
            p = flip(me_s, d)
            r, c = piece(p)
            remote(hid.at[h, r, c], by_time.at[h, me_s], p2_send.at[h], p2_recv.at[h], p, me_v).start()

    def filter_part(h):
        r, c = piece(me_s)
        by_time[h, me_s] = hid[h, r, c]
        pieces_arrived(h, n - 1, p2_recv.at[h])
        shift = 0 if across == 1 else (me_s % across) * piece_cols
        for i in range(0, piece_rows, 16):
            for j in range(0, piece_cols, 128):
                at = h * cols + j + shift
                if across > 1:
                    at = pl.multiple_of(at, 128)
                filt = taps[:, pl.ds(at, 128)]
                wide = [by_time[h, t, i : i + 16, j : j + 128].astype(F32) for t in range(n)]
                for t in range(n):
                    value = filt[0:1] * wide[t]
                    for k in range(1, min(filt.shape[0] - 1, t) + 1):
                        value = value + filt[k : k + 1] * wide[t - k]
                    mix[h, t, i : i + 16, j : j + 128] = value.astype(BF16)
        for d in order:
            p = flip(me_s, d)
            remote(
                mix.at[h, p], mixed.at[h, me_v, r, c], p3_send.at[h], p3_recv.at[h, d // (n // GROUPS)], p, me_v
            ).start()
        mixed[h, me_v, r, c] = mix[h, me_s]

    load_taps.wait()
    for h in range(parts):
        pass_on(h)
        near_messages(h)
        far_messages(h)
        if h >= 2:
            filter_part(h - 2)
    for h in range(max(0, parts - 2), parts):
        filter_part(h)

    half = rows // GROUPS
    size = n // GROUPS

    def group_rows(g):
        start = me_s // size if g == 0 else 1 - me_s // size
        return pl.ds(pl.multiple_of(start * half, half), half)

    def send_group(h, g):
        pieces_arrived(h, size if g else size - 1, p3_recv.at[h, g])
        block = mixed.at[h, me_v, group_rows(g)]
        for d in range(1, ny):
            go(block, block, y4_send.at[d, h, g], y4_recv.at[d, h, g], me_s, y_to(d))
        if g + 1 == GROUPS:
            block = mixed.at[h, me_v]
            go(block, block, s4_send.at[h], s4_recv.at[h], me_s, sib)

    def pass_group(h, g):
        for d in range(1, ny):
            src = y_from(d)
            block = mixed.at[h, src, group_rows(g)]
            remote(block, block, y4_send.at[d, h, g], y4_recv.at[d, h, g], me_s, src).wait_recv()
            go(block, block, f4_send.at[d, h, g], f4_recv.at[d, h, g], me_s, sib)

    def near_part(h):
        value = dot(dense[me_v], mixed[h, me_v])
        block = mixed.at[h, sib]
        remote(block, block, s4_send.at[h], s4_recv.at[h], me_s, sib).wait_recv()
        acc[:, lanes(h)] = value + dot(dense[sib], mixed[h, sib])
        own = dot(mixed[h, me_v], weights[2, lanes(h), :])
        if h == 0:
            total[...] = own
        else:
            total[...] += own

    def far_part(h):
        value = acc[:, lanes(h)]
        for d in range(1, ny):
            src = y_from(d)
            value = value + dot(dense[src], mixed[h, src])
        for d in range(1, ny):
            src = ((y - d + ny) % ny) * 2 + 1 - core
            for g in range(GROUPS):
                block = mixed.at[h, src, group_rows(g)]
                remote(block, block, f4_send.at[d, h, g], f4_recv.at[d, h, g], me_s, sib).wait_recv()
            value = value + dot(dense[src], mixed[h, src])
        last = dot(value.astype(BF16), weights[3, lanes(h), :])
        if h + 1 < parts:
            total[...] += last
        else:
            out[0] = (total[...] + last).astype(BF16)

    loads[2].wait()
    loads[3].wait()
    all_left()
    for h in range(parts):
        pieces_left(h, p2_send.at[h])
    send_group(0, 0)
    send_group(0, 1)
    for h in range(parts):
        pass_group(h, 0)
        if h + 1 < parts:
            send_group(h + 1, 0)
        if h > 0:
            far_part(h - 1)
            near_part(h)
        pass_group(h, 1)
        if h + 1 < parts:
            send_group(h + 1, 1)
            pieces_left(h, p3_send.at[h])
        if h == 0:
            near_part(h)
    far_part(parts - 1)
    pieces_left(parts - 1, p3_send.at[parts - 1])
    all_left()


def shards(n, nv, features, tile_values, tile_column, tile_count, *rest):
    _, rows, width = features.shape
    _, per, slots, tile, _ = tile_values.shape
    ny = nv // 2
    parts, cols, _, piece_rows, piece_cols = cut(n, rows, width)
    taps = rest[2].shape[0]
    dma = pltpu.SemaphoreType.DMA
    hbm = pl.BlockSpec(memory_space=pltpu.HBM)
    hold = [pltpu.with_memory_space_constraint(x, pltpu.HBM) for x in (features, tile_values, tile_column, tile_count, *rest)]
    summed = pl.pallas_call(
        functools.partial(kernel, (n, nv, rows, width, slots, tile)),
        out_shape=jax.ShapeDtypeStruct((1, rows, width), BF16),
        in_specs=[hbm] * 9,
        out_specs=pl.BlockSpec(memory_space=pltpu.VMEM),
        scratch_shapes=[
            pltpu.SMEM((per, slots), jnp.int32),
            pltpu.SMEM((1, per), jnp.int32),
            pltpu.VMEM((rows, width), BF16),
            pltpu.VMEM((parts, nv, rows, cols), BF16),
            pltpu.VMEM((per, slots, tile, tile), BF16),
            pltpu.VMEM((nv, rows, rows), BF16),
            pltpu.VMEM((4, width, width), BF16),
            pltpu.VMEM((taps, width), F32),
            pltpu.VMEM((rows, width), F32),
            pltpu.VMEM((rows, width), F32),
            pltpu.VMEM((parts, rows, cols), BF16),
            pltpu.VMEM((parts, n, piece_rows, piece_cols), BF16),
            pltpu.VMEM((parts, n, piece_rows, piece_cols), BF16),
            pltpu.VMEM((parts, nv, rows, cols), BF16),
            dma((9,)),
            dma((parts,)),
            dma((parts,)),
            dma((ny, parts)),
            dma((ny, parts)),
            dma((ny, parts)),
            dma((ny, parts)),
            dma((parts,)),
            dma((parts,)),
            dma((parts,)),
            dma((parts, GROUPS)),
            dma((ny, parts, GROUPS)),
            dma((ny, parts, GROUPS)),
            dma((parts,)),
            dma((parts,)),
            dma((ny, parts, GROUPS)),
            dma((ny, parts, GROUPS)),
        ],
        compiler_params=pltpu.CompilerParams(
            collective_id=0, has_side_effects=True, vmem_limit_bytes=40 * 1024 * 1024
        ),
    )(*hold)
    return jnp.maximum(summed, 0)


def solution(mesh):
    n, nv = mesh.shape["snap"], mesh.shape["vert"]
    return jax.shard_map(
        functools.partial(shards, n, nv),
        mesh=mesh,
        in_specs=(
            P("snap", "vert", None),
            P("snap", "vert", None, None, None),
            P("snap", "vert", None),
            P("snap", "vert"),
            P(),
            P(),
            P(),
            P(),
            P(),
        ),
        out_specs=P("snap", "vert", None),
        check_vma=False,
    )
```

```python
import functools

import jax
import jax.numpy as jnp
from jax import lax
from jax.experimental import pallas as pl
from jax.experimental.pallas import tpu as pltpu
from jax.sharding import PartitionSpec as P

MESH = pl.DeviceIdType.MESH
GROUPS = 2
MOST_PARTS = 2
F32 = jnp.float32
BF16 = jnp.bfloat16


def cut(n, rows, width):
    piece_rows = max(rows // n, 16)
    across = n // (rows // piece_rows)
    parts = max(1, min(MOST_PARTS, width // 128 // across))
    return parts, width // parts, across, piece_rows, width // parts // across


def flip(index, mask):
    out, bit = index, 1
    while bit <= mask:
        if mask & bit:
            out = out + (1 - 2 * ((index // bit) % 2)) * bit
        bit *= 2
    return out


def kernel(
    sizes,
    features,
    tile_values,
    columns,
    counts,
    message_one,
    root_one,
    time_taps,
    message_two,
    root_two,
    out,
    column_smem,
    count_smem,
    feats,
    msgs,
    tiles,
    dense,
    weights,
    taps,
    acc,
    total,
    hid,
    by_time,
    mix,
    mixed,
    local_sem,
    near_send,
    near_recv,
    y1_send,
    y1_recv,
    f1_send,
    f1_recv,
    p2_send,
    p2_recv,
    p3_send,
    p3_recv,
    y4_send,
    y4_recv,
    s4_send,
    s4_recv,
    f4_send,
    f4_recv,
):
    n, nv, rows, width, slots, tile = sizes
    ny = nv // 2
    per = rows // tile
    parts, cols, across, piece_rows, piece_cols = cut(n, rows, width)
    me_s, me_v = lax.axis_index("snap"), lax.axis_index("vert")
    y, core = me_v // 2, me_v % 2
    sib = y * 2 + 1 - core

    def piece(p):
        r = pl.multiple_of((p // across) * piece_rows, piece_rows)
        if across == 1:
            return pl.ds(r, piece_rows), slice(0, piece_cols)
        return pl.ds(r, piece_rows), pl.ds(pl.multiple_of((p % across) * piece_cols, piece_cols), piece_cols)

    def remote(src, dst, send, recv, s, v):
        return pltpu.make_async_remote_copy(
            src_ref=src, dst_ref=dst, send_sem=send, recv_sem=recv, device_id=(s, v), device_id_type=MESH
        )

    sent = []

    def go(*args):
        copy = remote(*args)
        copy.start()
        sent.append(copy)

    def pieces_arrived(h, count, recv):
        block = by_time.at[h, pl.ds(0, count)]
        remote(block, block, recv, recv, me_s, sib).wait_recv()

    def pieces_left(h, send):
        block = by_time.at[h, pl.ds(0, n - 1)]
        remote(block, block, send, send, me_s, sib).wait_send()

    def all_left():
        for copy in sent:
            copy.wait_send()
        sent.clear()

    def y_to(d):
        return ((y + d) % ny) * 2 + core

    def y_from(d):
        return ((y - d + ny) % ny) * 2 + core

    load_feats = pltpu.make_async_copy(features.at[0], feats, local_sem.at[0])
    load_tiles = pltpu.make_async_copy(tile_values.at[0], tiles, local_sem.at[1])
    loads = [
        pltpu.make_async_copy(ref, weights.at[i], local_sem.at[2 + i])
        for i, ref in enumerate((root_one, message_one, root_two, message_two))
    ]
    load_taps = pltpu.make_async_copy(time_taps, taps, local_sem.at[6])
    load_columns = pltpu.make_async_copy(columns.at[0], column_smem, local_sem.at[7])
    load_counts = pltpu.make_async_copy(counts, count_smem, local_sem.at[8])
    load_feats.start()
    loads[1].start()
    barrier = pltpu.get_barrier_semaphore()
    for d in range(1, n):
        pl.semaphore_signal(barrier, inc=1, device_id=(flip(me_s, d), me_v), device_id_type=MESH)
    for d in range(1, ny):
        pl.semaphore_signal(barrier, inc=1, device_id=(me_s, y_to(d)), device_id_type=MESH)
    pl.semaphore_signal(barrier, inc=1, device_id=(me_s, sib), device_id_type=MESH)
    for load in (load_columns, load_counts, load_tiles, loads[0], load_taps, loads[2], loads[3]):
        load.start()

    def dot(a, b):
        return jnp.dot(a, b, preferred_element_type=F32)

    def lanes(h):
        return slice(h * cols, (h + 1) * cols)

    load_feats.wait()
    loads[1].wait()
    for h in range(parts):
        msgs[h, me_v] = dot(feats[...], weights[1, :, lanes(h)]).astype(BF16)
        if h == 0:
            pl.semaphore_wait(barrier, n - 1 + ny)
        block = msgs.at[h, me_v]
        for d in range(1, ny):
            go(block, block, y1_send.at[d, h], y1_recv.at[d, h], me_s, y_to(d))
        go(block, block, near_send.at[h], near_recv.at[h], me_s, sib)

    def pass_on(h):
        for d in range(1, ny):
            src = y_from(d)
            block = msgs.at[h, src]
            remote(block, block, y1_send.at[d, h], y1_recv.at[d, h], me_s, src).wait_recv()
            go(block, block, f1_send.at[d, h], f1_recv.at[d, h], me_s, sib)

    load_columns.wait()
    load_counts.wait()
    load_tiles.wait()
    live = [
        [jnp.where(k < count_smem[0, b], column_smem[b, k], -1) for k in range(slots)] for b in range(per)
    ]

    def fill(i, carry):
        v = ((y - i // 2 + ny) % ny) * 2 + (core + i) % 2
        for b in range(per):
            for j in range(per):
                block = jnp.zeros((tile, tile), F32)
                for k in range(slots):
                    scale = jnp.where(live[b][k] == v * per + j, 1.0, 0.0).astype(F32)
                    block = block + scale * tiles[b, k].astype(F32)
                dense[v, b * tile : (b + 1) * tile, j * tile : (j + 1) * tile] = block.astype(BF16)
        return carry

    lax.fori_loop(0, 2, fill, 0)

    order = list(range(n // 2, n)) + list(range(1, n // 2))
    loads[0].wait()

    def near_messages(h):
        total[:, lanes(h)] = dot(feats[...], weights[0, :, lanes(h)])
        block = msgs.at[h, sib]
        remote(block, block, near_send.at[h], near_recv.at[h], me_s, sib).wait_recv()
        total[:, lanes(h)] += dot(dense[me_v], msgs[h, me_v]) + dot(dense[sib], msgs[h, sib])

    def far_messages(h):
        value = total[:, lanes(h)]
        for d in range(1, ny):
            src = y_from(d)
            value = value + dot(dense[src], msgs[h, src])
        for d in range(1, ny):
            src = ((y - d + ny) % ny) * 2 + 1 - core
            block = msgs.at[h, src]
            remote(block, block, f1_send.at[d, h], f1_recv.at[d, h], me_s, sib).wait_recv()
            value = value + dot(dense[src], msgs[h, src])
        hid[h] = jnp.maximum(value, 0.0).astype(BF16)
        for d in order:
            p = flip(me_s, d)
            r, c = piece(p)
            remote(hid.at[h, r, c], by_time.at[h, me_s], p2_send.at[h], p2_recv.at[h], p, me_v).start()

    def filter_part(h):
        r, c = piece(me_s)
        by_time[h, me_s] = hid[h, r, c]
        pieces_arrived(h, n - 1, p2_recv.at[h])
        shift = 0 if across == 1 else (me_s % across) * piece_cols
        for i in range(0, piece_rows, 16):
            for j in range(0, piece_cols, 128):
                at = h * cols + j + shift
                if across > 1:
                    at = pl.multiple_of(at, 128)
                filt = taps[:, pl.ds(at, 128)]
                wide = [by_time[h, t, i : i + 16, j : j + 128].astype(F32) for t in range(n)]
                for t in range(n):
                    value = filt[0:1] * wide[t]
                    for k in range(1, min(filt.shape[0] - 1, t) + 1):
                        value = value + filt[k : k + 1] * wide[t - k]
                    mix[h, t, i : i + 16, j : j + 128] = value.astype(BF16)
        for d in order:
            p = flip(me_s, d)
            remote(
                mix.at[h, p], mixed.at[h, me_v, r, c], p3_send.at[h], p3_recv.at[h, d // (n // GROUPS)], p, me_v
            ).start()
        mixed[h, me_v, r, c] = mix[h, me_s]

    load_taps.wait()
    for h in range(parts):
        pass_on(h)
        if h == 0:
            lax.fori_loop(2, nv, fill, 0)
        near_messages(h)
        far_messages(h)
        if h >= 2:
            filter_part(h - 2)
    for h in range(max(0, parts - 2), parts):
        filter_part(h)

    half = rows // GROUPS
    size = n // GROUPS

    def group_rows(g):
        start = me_s // size if g == 0 else 1 - me_s // size
        return pl.ds(pl.multiple_of(start * half, half), half)

    def send_group(h, g):
        pieces_arrived(h, size if g else size - 1, p3_recv.at[h, g])
        block = mixed.at[h, me_v, group_rows(g)]
        for d in range(1, ny):
            go(block, block, y4_send.at[d, h, g], y4_recv.at[d, h, g], me_s, y_to(d))
        if g + 1 == GROUPS:
            block = mixed.at[h, me_v]
            go(block, block, s4_send.at[h], s4_recv.at[h], me_s, sib)

    def pass_group(h, g):
        for d in range(1, ny):
            src = y_from(d)
            block = mixed.at[h, src, group_rows(g)]
            remote(block, block, y4_send.at[d, h, g], y4_recv.at[d, h, g], me_s, src).wait_recv()
            go(block, block, f4_send.at[d, h, g], f4_recv.at[d, h, g], me_s, sib)

    def near_part(h):
        value = dot(dense[me_v], mixed[h, me_v])
        block = mixed.at[h, sib]
        remote(block, block, s4_send.at[h], s4_recv.at[h], me_s, sib).wait_recv()
        acc[:, lanes(h)] = value + dot(dense[sib], mixed[h, sib])
        own = dot(mixed[h, me_v], weights[2, lanes(h), :])
        if h == 0:
            total[...] = own
        else:
            total[...] += own

    def far_part(h):
        value = acc[:, lanes(h)]
        for d in range(1, ny):
            src = y_from(d)
            value = value + dot(dense[src], mixed[h, src])
        for d in range(1, ny):
            src = ((y - d + ny) % ny) * 2 + 1 - core
            for g in range(GROUPS):
                block = mixed.at[h, src, group_rows(g)]
                remote(block, block, f4_send.at[d, h, g], f4_recv.at[d, h, g], me_s, sib).wait_recv()
            value = value + dot(dense[src], mixed[h, src])
        last = dot(value.astype(BF16), weights[3, lanes(h), :])
        if h + 1 < parts:
            total[...] += last
        else:
            out[0] = (total[...] + last).astype(BF16)

    loads[2].wait()
    loads[3].wait()
    all_left()
    for h in range(parts):
        pieces_left(h, p2_send.at[h])
    send_group(0, 0)
    send_group(0, 1)
    for h in range(parts):
        pass_group(h, 0)
        if h + 1 < parts:
            send_group(h + 1, 0)
        if h > 0:
            far_part(h - 1)
        pass_group(h, 1)
        if h + 1 < parts:
            send_group(h + 1, 1)
            pieces_left(h, p3_send.at[h])
        near_part(h)
    far_part(parts - 1)
    pieces_left(parts - 1, p3_send.at[parts - 1])
    all_left()


def shards(n, nv, features, tile_values, tile_column, tile_count, *rest):
    _, rows, width = features.shape
    _, per, slots, tile, _ = tile_values.shape
    ny = nv // 2
    parts, cols, _, piece_rows, piece_cols = cut(n, rows, width)
    taps = rest[2].shape[0]
    dma = pltpu.SemaphoreType.DMA
    hbm = pl.BlockSpec(memory_space=pltpu.HBM)
    hold = [pltpu.with_memory_space_constraint(x, pltpu.HBM) for x in (features, tile_values, tile_column, tile_count, *rest)]
    summed = pl.pallas_call(
        functools.partial(kernel, (n, nv, rows, width, slots, tile)),
        out_shape=jax.ShapeDtypeStruct((1, rows, width), BF16),
        in_specs=[hbm] * 9,
        out_specs=pl.BlockSpec(memory_space=pltpu.VMEM),
        scratch_shapes=[
            pltpu.SMEM((per, slots), jnp.int32),
            pltpu.SMEM((1, per), jnp.int32),
            pltpu.VMEM((rows, width), BF16),
            pltpu.VMEM((parts, nv, rows, cols), BF16),
            pltpu.VMEM((per, slots, tile, tile), BF16),
            pltpu.VMEM((nv, rows, rows), BF16),
            pltpu.VMEM((4, width, width), BF16),
            pltpu.VMEM((taps, width), F32),
            pltpu.VMEM((rows, width), F32),
            pltpu.VMEM((rows, width), F32),
            pltpu.VMEM((parts, rows, cols), BF16),
            pltpu.VMEM((parts, n, piece_rows, piece_cols), BF16),
            pltpu.VMEM((parts, n, piece_rows, piece_cols), BF16),
            pltpu.VMEM((parts, nv, rows, cols), BF16),
            dma((9,)),
            dma((parts,)),
            dma((parts,)),
            dma((ny, parts)),
            dma((ny, parts)),
            dma((ny, parts)),
            dma((ny, parts)),
            dma((parts,)),
            dma((parts,)),
            dma((parts,)),
            dma((parts, GROUPS)),
            dma((ny, parts, GROUPS)),
            dma((ny, parts, GROUPS)),
            dma((parts,)),
            dma((parts,)),
            dma((ny, parts, GROUPS)),
            dma((ny, parts, GROUPS)),
        ],
        compiler_params=pltpu.CompilerParams(
            collective_id=0, has_side_effects=True, vmem_limit_bytes=40 * 1024 * 1024
        ),
    )(*hold)
    return jnp.maximum(summed, 0)


def solution(mesh):
    n, nv = mesh.shape["snap"], mesh.shape["vert"]
    return jax.shard_map(
        functools.partial(shards, n, nv),
        mesh=mesh,
        in_specs=(
            P("snap", "vert", None),
            P("snap", "vert", None, None, None),
            P("snap", "vert", None),
            P("snap", "vert"),
            P(),
            P(),
            P(),
            P(),
            P(),
        ),
        out_specs=P("snap", "vert", None),
        check_vma=False,
    )
```

```python
import functools

import jax
import jax.numpy as jnp
from jax import lax
from jax.experimental import pallas as pl
from jax.experimental.pallas import tpu as pltpu
from jax.sharding import PartitionSpec as P

MESH = pl.DeviceIdType.MESH
GROUPS = 4
MOST_PARTS = 2
F32 = jnp.float32
BF16 = jnp.bfloat16


def cut(n, rows, width):
    piece_rows = max(rows // n, 16)
    across = n // (rows // piece_rows)
    parts = max(1, min(MOST_PARTS, width // 128 // across))
    return parts, width // parts, across, piece_rows, width // parts // across


def flip(index, mask):
    out, bit = index, 1
    while bit <= mask:
        if mask & bit:
            out = out + (1 - 2 * ((index // bit) % 2)) * bit
        bit *= 2
    return out


def kernel(
    sizes,
    features,
    tile_values,
    columns,
    counts,
    message_one,
    root_one,
    time_taps,
    message_two,
    root_two,
    out,
    column_smem,
    count_smem,
    feats,
    msgs,
    tiles,
    dense,
    weights,
    taps,
    acc,
    total,
    hid,
    by_time,
    mix,
    mixed,
    local_sem,
    near_send,
    near_recv,
    y1_send,
    y1_recv,
    f1_send,
    f1_recv,
    p2_send,
    p2_recv,
    p3_send,
    p3_recv,
    y4_send,
    y4_recv,
    s4_send,
    s4_recv,
    f4_send,
    f4_recv,
):
    n, nv, rows, width, slots, tile = sizes
    ny = nv // 2
    per = rows // tile
    parts, cols, across, piece_rows, piece_cols = cut(n, rows, width)
    me_s, me_v = lax.axis_index("snap"), lax.axis_index("vert")
    y, core = me_v // 2, me_v % 2
    sib = y * 2 + 1 - core

    def piece(p):
        r = pl.multiple_of((p // across) * piece_rows, piece_rows)
        if across == 1:
            return pl.ds(r, piece_rows), slice(0, piece_cols)
        return pl.ds(r, piece_rows), pl.ds(pl.multiple_of((p % across) * piece_cols, piece_cols), piece_cols)

    def remote(src, dst, send, recv, s, v):
        return pltpu.make_async_remote_copy(
            src_ref=src, dst_ref=dst, send_sem=send, recv_sem=recv, device_id=(s, v), device_id_type=MESH
        )

    sent = []

    def go(*args):
        copy = remote(*args)
        copy.start()
        sent.append(copy)

    def pieces_arrived(h, count, recv):
        block = by_time.at[h, pl.ds(0, count)]
        remote(block, block, recv, recv, me_s, sib).wait_recv()

    def pieces_left(h, send):
        block = by_time.at[h, pl.ds(0, n - 1)]
        remote(block, block, send, send, me_s, sib).wait_send()

    def all_left():
        for copy in sent:
            copy.wait_send()
        sent.clear()

    def y_to(d):
        return ((y + d) % ny) * 2 + core

    def y_from(d):
        return ((y - d + ny) % ny) * 2 + core

    load_feats = pltpu.make_async_copy(features.at[0], feats, local_sem.at[0])
    load_tiles = pltpu.make_async_copy(tile_values.at[0], tiles, local_sem.at[1])
    loads = [
        pltpu.make_async_copy(ref, weights.at[i], local_sem.at[2 + i])
        for i, ref in enumerate((root_one, message_one, root_two, message_two))
    ]
    load_taps = pltpu.make_async_copy(time_taps, taps, local_sem.at[6])
    load_columns = pltpu.make_async_copy(columns.at[0], column_smem, local_sem.at[7])
    load_counts = pltpu.make_async_copy(counts, count_smem, local_sem.at[8])
    load_feats.start()
    loads[1].start()
    barrier = pltpu.get_barrier_semaphore()
    for d in range(1, n):
        pl.semaphore_signal(barrier, inc=1, device_id=(flip(me_s, d), me_v), device_id_type=MESH)
    for d in range(1, ny):
        pl.semaphore_signal(barrier, inc=1, device_id=(me_s, y_to(d)), device_id_type=MESH)
    pl.semaphore_signal(barrier, inc=1, device_id=(me_s, sib), device_id_type=MESH)
    for load in (load_columns, load_counts, load_tiles, loads[0], load_taps, loads[2], loads[3]):
        load.start()

    def dot(a, b):
        return jnp.dot(a, b, preferred_element_type=F32)

    def lanes(h):
        return slice(h * cols, (h + 1) * cols)

    load_feats.wait()
    loads[1].wait()
    for h in range(parts):
        msgs[h, me_v] = dot(feats[...], weights[1, :, lanes(h)]).astype(BF16)
        if h == 0:
            pl.semaphore_wait(barrier, n - 1 + ny)
        block = msgs.at[h, me_v]
        for d in range(1, ny):
            go(block, block, y1_send.at[d, h], y1_recv.at[d, h], me_s, y_to(d))
        go(block, block, near_send.at[h], near_recv.at[h], me_s, sib)

    def pass_on(h):
        for d in range(1, ny):
            src = y_from(d)
            block = msgs.at[h, src]
            remote(block, block, y1_send.at[d, h], y1_recv.at[d, h], me_s, src).wait_recv()
            go(block, block, f1_send.at[d, h], f1_recv.at[d, h], me_s, sib)

    load_columns.wait()
    load_counts.wait()
    load_tiles.wait()
    live = [
        [jnp.where(k < count_smem[0, b], column_smem[b, k], -1) for k in range(slots)] for b in range(per)
    ]

    def fill(i, carry):
        v = ((y - i // 2 + ny) % ny) * 2 + (core + i) % 2
        for b in range(per):
            for j in range(per):
                block = jnp.zeros((tile, tile), F32)
                for k in range(slots):
                    scale = jnp.where(live[b][k] == v * per + j, 1.0, 0.0).astype(F32)
                    block = block + scale * tiles[b, k].astype(F32)
                dense[v, b * tile : (b + 1) * tile, j * tile : (j + 1) * tile] = block.astype(BF16)
        return carry

    lax.fori_loop(0, 2, fill, 0)

    order = list(range(n // 2, n)) + list(range(1, n // 2))
    loads[0].wait()

    def near_messages(h):
        total[:, lanes(h)] = dot(feats[...], weights[0, :, lanes(h)])
        block = msgs.at[h, sib]
        remote(block, block, near_send.at[h], near_recv.at[h], me_s, sib).wait_recv()
        total[:, lanes(h)] += dot(dense[me_v], msgs[h, me_v]) + dot(dense[sib], msgs[h, sib])

    def far_messages(h):
        value = total[:, lanes(h)]
        for d in range(1, ny):
            src = y_from(d)
            value = value + dot(dense[src], msgs[h, src])
        for d in range(1, ny):
            src = ((y - d + ny) % ny) * 2 + 1 - core
            block = msgs.at[h, src]
            remote(block, block, f1_send.at[d, h], f1_recv.at[d, h], me_s, sib).wait_recv()
            value = value + dot(dense[src], msgs[h, src])
        hid[h] = jnp.maximum(value, 0.0).astype(BF16)
        for d in order:
            p = flip(me_s, d)
            r, c = piece(p)
            remote(hid.at[h, r, c], by_time.at[h, me_s], p2_send.at[h], p2_recv.at[h], p, me_v).start()

    def filter_part(h):
        r, c = piece(me_s)
        by_time[h, me_s] = hid[h, r, c]
        pieces_arrived(h, n - 1, p2_recv.at[h])
        shift = 0 if across == 1 else (me_s % across) * piece_cols
        for i in range(0, piece_rows, 16):
            for j in range(0, piece_cols, 128):
                at = h * cols + j + shift
                if across > 1:
                    at = pl.multiple_of(at, 128)
                filt = taps[:, pl.ds(at, 128)]
                wide = [by_time[h, t, i : i + 16, j : j + 128].astype(F32) for t in range(n)]
                for t in range(n):
                    value = filt[0:1] * wide[t]
                    for k in range(1, min(filt.shape[0] - 1, t) + 1):
                        value = value + filt[k : k + 1] * wide[t - k]
                    mix[h, t, i : i + 16, j : j + 128] = value.astype(BF16)
        for d in order:
            p = flip(me_s, d)
            remote(
                mix.at[h, p], mixed.at[h, me_v, r, c], p3_send.at[h], p3_recv.at[h, d // (n // GROUPS)], p, me_v
            ).start()
        mixed[h, me_v, r, c] = mix[h, me_s]

    load_taps.wait()
    for h in range(parts):
        pass_on(h)
        if h == 0:
            lax.fori_loop(2, nv, fill, 0)
        near_messages(h)
        far_messages(h)
        if h >= 2:
            filter_part(h - 2)
    for h in range(max(0, parts - 2), parts):
        filter_part(h)

    half = rows // GROUPS
    size = n // GROUPS

    def group_rows(g):
        start = flip(me_s // size, g)
        return pl.ds(pl.multiple_of(start * half, half), half)

    def send_group(h, g):
        pieces_arrived(h, size if g else size - 1, p3_recv.at[h, g])
        block = mixed.at[h, me_v, group_rows(g)]
        for d in range(1, ny):
            go(block, block, y4_send.at[d, h, g], y4_recv.at[d, h, g], me_s, y_to(d))
        if g + 1 == GROUPS:
            block = mixed.at[h, me_v]
            go(block, block, s4_send.at[h], s4_recv.at[h], me_s, sib)

    def pass_group(h, g):
        for d in range(1, ny):
            src = y_from(d)
            block = mixed.at[h, src, group_rows(g)]
            remote(block, block, y4_send.at[d, h, g], y4_recv.at[d, h, g], me_s, src).wait_recv()
            go(block, block, f4_send.at[d, h, g], f4_recv.at[d, h, g], me_s, sib)

    def near_part(h):
        value = dot(dense[me_v], mixed[h, me_v])
        block = mixed.at[h, sib]
        remote(block, block, s4_send.at[h], s4_recv.at[h], me_s, sib).wait_recv()
        acc[:, lanes(h)] = value + dot(dense[sib], mixed[h, sib])
        own = dot(mixed[h, me_v], weights[2, lanes(h), :])
        if h == 0:
            total[...] = own
        else:
            total[...] += own

    def far_part(h):
        value = acc[:, lanes(h)]
        for d in range(1, ny):
            src = y_from(d)
            value = value + dot(dense[src], mixed[h, src])
        for d in range(1, ny):
            src = ((y - d + ny) % ny) * 2 + 1 - core
            for g in range(GROUPS):
                block = mixed.at[h, src, group_rows(g)]
                remote(block, block, f4_send.at[d, h, g], f4_recv.at[d, h, g], me_s, sib).wait_recv()
            value = value + dot(dense[src], mixed[h, src])
        last = dot(value.astype(BF16), weights[3, lanes(h), :])
        if h + 1 < parts:
            total[...] += last
        else:
            out[0] = (total[...] + last).astype(BF16)

    loads[2].wait()
    loads[3].wait()
    all_left()
    for h in range(parts):
        pieces_left(h, p2_send.at[h])
    steps = [(h, g) for h in range(parts) for g in range(GROUPS)]
    for i in range(len(steps) + 2):
        if i < len(steps):
            send_group(*steps[i])
        if i >= 2:
            h, g = steps[i - 2]
            pass_group(h, g)
            if g + 1 == GROUPS:
                near_part(h)
            elif g == 1 and h > 0:
                far_part(h - 1)
                pieces_left(h - 1, p3_send.at[h - 1])
    far_part(parts - 1)
    pieces_left(parts - 1, p3_send.at[parts - 1])
    all_left()


def shards(n, nv, features, tile_values, tile_column, tile_count, *rest):
    _, rows, width = features.shape
    _, per, slots, tile, _ = tile_values.shape
    ny = nv // 2
    parts, cols, _, piece_rows, piece_cols = cut(n, rows, width)
    taps = rest[2].shape[0]
    dma = pltpu.SemaphoreType.DMA
    hbm = pl.BlockSpec(memory_space=pltpu.HBM)
    hold = [pltpu.with_memory_space_constraint(x, pltpu.HBM) for x in (features, tile_values, tile_column, tile_count, *rest)]
    summed = pl.pallas_call(
        functools.partial(kernel, (n, nv, rows, width, slots, tile)),
        out_shape=jax.ShapeDtypeStruct((1, rows, width), BF16),
        in_specs=[hbm] * 9,
        out_specs=pl.BlockSpec(memory_space=pltpu.VMEM),
        scratch_shapes=[
            pltpu.SMEM((per, slots), jnp.int32),
            pltpu.SMEM((1, per), jnp.int32),
            pltpu.VMEM((rows, width), BF16),
            pltpu.VMEM((parts, nv, rows, cols), BF16),
            pltpu.VMEM((per, slots, tile, tile), BF16),
            pltpu.VMEM((nv, rows, rows), BF16),
            pltpu.VMEM((4, width, width), BF16),
            pltpu.VMEM((taps, width), F32),
            pltpu.VMEM((rows, width), F32),
            pltpu.VMEM((rows, width), F32),
            pltpu.VMEM((parts, rows, cols), BF16),
            pltpu.VMEM((parts, n, piece_rows, piece_cols), BF16),
            pltpu.VMEM((parts, n, piece_rows, piece_cols), BF16),
            pltpu.VMEM((parts, nv, rows, cols), BF16),
            dma((9,)),
            dma((parts,)),
            dma((parts,)),
            dma((ny, parts)),
            dma((ny, parts)),
            dma((ny, parts)),
            dma((ny, parts)),
            dma((parts,)),
            dma((parts,)),
            dma((parts,)),
            dma((parts, GROUPS)),
            dma((ny, parts, GROUPS)),
            dma((ny, parts, GROUPS)),
            dma((parts,)),
            dma((parts,)),
            dma((ny, parts, GROUPS)),
            dma((ny, parts, GROUPS)),
        ],
        compiler_params=pltpu.CompilerParams(
            collective_id=0, has_side_effects=True, vmem_limit_bytes=40 * 1024 * 1024
        ),
    )(*hold)
    return jnp.maximum(summed, 0)


def solution(mesh):
    n, nv = mesh.shape["snap"], mesh.shape["vert"]
    return jax.shard_map(
        functools.partial(shards, n, nv),
        mesh=mesh,
        in_specs=(
            P("snap", "vert", None),
            P("snap", "vert", None, None, None),
            P("snap", "vert", None),
            P("snap", "vert"),
            P(),
            P(),
            P(),
            P(),
            P(),
        ),
        out_specs=P("snap", "vert", None),
        check_vma=False,
    )
```

```python
import functools

import jax
import jax.numpy as jnp
from jax import lax
from jax.experimental import pallas as pl
from jax.experimental.pallas import tpu as pltpu
from jax.sharding import PartitionSpec as P

MESH = pl.DeviceIdType.MESH
GROUPS = 2
MOST_PARTS = 2
F32 = jnp.float32
BF16 = jnp.bfloat16


def cut(n, rows, width):
    piece_rows = max(rows // n, 16)
    across = n // (rows // piece_rows)
    parts = max(1, min(MOST_PARTS, width // 128 // across))
    return parts, width // parts, across, piece_rows, width // parts // across


def flip(index, mask):
    out, bit = index, 1
    while bit <= mask:
        if mask & bit:
            out = out + (1 - 2 * ((index // bit) % 2)) * bit
        bit *= 2
    return out


def kernel(
    sizes,
    features,
    tile_values,
    columns,
    counts,
    message_one,
    root_one,
    time_taps,
    message_two,
    root_two,
    out,
    column_smem,
    count_smem,
    feats,
    msgs,
    tiles,
    dense,
    weights,
    taps,
    acc,
    total,
    hid,
    by_time,
    mix,
    mixed,
    local_sem,
    near_send,
    near_recv,
    y1_send,
    y1_recv,
    f1_send,
    f1_recv,
    p2_send,
    p2_recv,
    p3_send,
    p3_recv,
    y4_send,
    y4_recv,
    s4_send,
    s4_recv,
    f4_send,
    f4_recv,
):
    n, nv, rows, width, slots, tile = sizes
    ny = nv // 2
    per = rows // tile
    parts, cols, across, piece_rows, piece_cols = cut(n, rows, width)
    me_s, me_v = lax.axis_index("snap"), lax.axis_index("vert")
    y, core = me_v // 2, me_v % 2
    sib = y * 2 + 1 - core

    def piece(p):
        r = pl.multiple_of((p // across) * piece_rows, piece_rows)
        if across == 1:
            return pl.ds(r, piece_rows), slice(0, piece_cols)
        return pl.ds(r, piece_rows), pl.ds(pl.multiple_of((p % across) * piece_cols, piece_cols), piece_cols)

    def remote(src, dst, send, recv, s, v):
        return pltpu.make_async_remote_copy(
            src_ref=src, dst_ref=dst, send_sem=send, recv_sem=recv, device_id=(s, v), device_id_type=MESH
        )

    sent = []

    def go(*args):
        copy = remote(*args)
        copy.start()
        sent.append(copy)

    def pieces_arrived(h, count, recv):
        block = by_time.at[h, pl.ds(0, count)]
        remote(block, block, recv, recv, me_s, sib).wait_recv()

    def pieces_left(h, send):
        block = by_time.at[h, pl.ds(0, n - 1)]
        remote(block, block, send, send, me_s, sib).wait_send()

    def all_left():
        for copy in sent:
            copy.wait_send()
        sent.clear()

    def y_to(d):
        return ((y + d) % ny) * 2 + core

    def y_from(d):
        return ((y - d + ny) % ny) * 2 + core

    load_feats = pltpu.make_async_copy(features.at[0], feats, local_sem.at[0])
    load_tiles = pltpu.make_async_copy(tile_values.at[0], tiles, local_sem.at[1])
    loads = [
        pltpu.make_async_copy(ref, weights.at[i], local_sem.at[2 + i])
        for i, ref in enumerate((root_one, message_one, root_two, message_two))
    ]
    load_taps = pltpu.make_async_copy(time_taps, taps, local_sem.at[6])
    load_columns = pltpu.make_async_copy(columns.at[0], column_smem, local_sem.at[7])
    load_counts = pltpu.make_async_copy(counts, count_smem, local_sem.at[8])
    load_feats.start()
    loads[1].start()
    barrier = pltpu.get_barrier_semaphore()
    for d in range(1, n):
        pl.semaphore_signal(barrier, inc=1, device_id=(flip(me_s, d), me_v), device_id_type=MESH)
    for d in range(1, ny):
        pl.semaphore_signal(barrier, inc=1, device_id=(me_s, y_to(d)), device_id_type=MESH)
    pl.semaphore_signal(barrier, inc=1, device_id=(me_s, sib), device_id_type=MESH)
    for load in (load_columns, load_counts, load_tiles, loads[0], load_taps, loads[2], loads[3]):
        load.start()

    def dot(a, b):
        return jnp.dot(a, b, preferred_element_type=F32)

    def lanes(h):
        return slice(h * cols, (h + 1) * cols)

    load_feats.wait()
    loads[1].wait()
    for h in range(parts):
        msgs[h, me_v] = dot(feats[...], weights[1, :, lanes(h)]).astype(BF16)
        if h == 0:
            pl.semaphore_wait(barrier, n - 1 + ny)
        block = msgs.at[h, me_v]
        for d in range(1, ny):
            go(block, block, y1_send.at[d, h], y1_recv.at[d, h], me_s, y_to(d))
        go(block, block, near_send.at[h], near_recv.at[h], me_s, sib)

    def pass_on(h):
        for d in range(1, ny):
            src = y_from(d)
            block = msgs.at[h, src]
            remote(block, block, y1_send.at[d, h], y1_recv.at[d, h], me_s, src).wait_recv()
            go(block, block, f1_send.at[d, h], f1_recv.at[d, h], me_s, sib)

    load_columns.wait()
    load_counts.wait()
    load_tiles.wait()
    live = [
        [jnp.where(k < count_smem[0, b], column_smem[b, k], -1) for k in range(slots)] for b in range(per)
    ]

    def fill(i, carry):
        v = ((y - i // 2 + ny) % ny) * 2 + (core + i) % 2
        for b in range(per):
            for j in range(per):
                block = jnp.zeros((tile, tile), F32)
                for k in range(0, slots, 2):
                    pair = jnp.zeros((tile, tile), BF16)
                    for m in range(k, min(k + 2, slots)):
                        scale = jnp.where(live[b][m] == v * per + j, 1.0, 0.0).astype(F32)
                        pair = pair + jnp.full((tile, tile), scale, F32).astype(BF16) * tiles[b, m]
                    block = block + pair.astype(F32)
                dense[v, b * tile : (b + 1) * tile, j * tile : (j + 1) * tile] = block.astype(BF16)
        return carry

    lax.fori_loop(0, 2, fill, 0)

    order = list(range(n // 2, n)) + list(range(1, n // 2))
    loads[0].wait()

    def near_messages(h):
        total[:, lanes(h)] = dot(feats[...], weights[0, :, lanes(h)])
        block = msgs.at[h, sib]
        remote(block, block, near_send.at[h], near_recv.at[h], me_s, sib).wait_recv()
        total[:, lanes(h)] += dot(dense[me_v], msgs[h, me_v]) + dot(dense[sib], msgs[h, sib])

    def far_messages(h):
        value = total[:, lanes(h)]
        for d in range(1, ny):
            src = y_from(d)
            value = value + dot(dense[src], msgs[h, src])
        for d in range(1, ny):
            src = ((y - d + ny) % ny) * 2 + 1 - core
            block = msgs.at[h, src]
            remote(block, block, f1_send.at[d, h], f1_recv.at[d, h], me_s, sib).wait_recv()
            value = value + dot(dense[src], msgs[h, src])
        hid[h] = jnp.maximum(value, 0.0).astype(BF16)
        for d in order:
            p = flip(me_s, d)
            r, c = piece(p)
            remote(hid.at[h, r, c], by_time.at[h, me_s], p2_send.at[h], p2_recv.at[h], p, me_v).start()

    def filter_part(h):
        r, c = piece(me_s)
        by_time[h, me_s] = hid[h, r, c]
        pieces_arrived(h, n - 1, p2_recv.at[h])
        shift = 0 if across == 1 else (me_s % across) * piece_cols
        for i in range(0, piece_rows, 16):
            for j in range(0, piece_cols, 128):
                at = h * cols + j + shift
                if across > 1:
                    at = pl.multiple_of(at, 128)
                filt = taps[:, pl.ds(at, 128)]
                wide = [by_time[h, t, i : i + 16, j : j + 128].astype(F32) for t in range(n)]
                for t in range(n):
                    value = filt[0:1] * wide[t]
                    for k in range(1, min(filt.shape[0] - 1, t) + 1):
                        value = value + filt[k : k + 1] * wide[t - k]
                    mix[h, t, i : i + 16, j : j + 128] = value.astype(BF16)
        for d in order:
            p = flip(me_s, d)
            remote(
                mix.at[h, p], mixed.at[h, me_v, r, c], p3_send.at[h], p3_recv.at[h, d // (n // GROUPS)], p, me_v
            ).start()
        mixed[h, me_v, r, c] = mix[h, me_s]

    load_taps.wait()
    for h in range(parts):
        pass_on(h)
        if h == 0:
            lax.fori_loop(2, nv, fill, 0)
        near_messages(h)
        far_messages(h)
        if h >= 2:
            filter_part(h - 2)
    for h in range(max(0, parts - 2), parts):
        filter_part(h)

    half = rows // GROUPS
    size = n // GROUPS

    def group_rows(g):
        start = me_s // size if g == 0 else 1 - me_s // size
        return pl.ds(pl.multiple_of(start * half, half), half)

    def send_group(h, g):
        pieces_arrived(h, size if g else size - 1, p3_recv.at[h, g])
        block = mixed.at[h, me_v, group_rows(g)]
        for d in range(1, ny):
            go(block, block, y4_send.at[d, h, g], y4_recv.at[d, h, g], me_s, y_to(d))
        if g + 1 == GROUPS:
            block = mixed.at[h, me_v]
            go(block, block, s4_send.at[h], s4_recv.at[h], me_s, sib)

    def pass_group(h, g):
        for d in range(1, ny):
            src = y_from(d)
            block = mixed.at[h, src, group_rows(g)]
            remote(block, block, y4_send.at[d, h, g], y4_recv.at[d, h, g], me_s, src).wait_recv()
            go(block, block, f4_send.at[d, h, g], f4_recv.at[d, h, g], me_s, sib)

    def near_part(h):
        value = dot(dense[me_v], mixed[h, me_v])
        block = mixed.at[h, sib]
        remote(block, block, s4_send.at[h], s4_recv.at[h], me_s, sib).wait_recv()
        acc[:, lanes(h)] = value + dot(dense[sib], mixed[h, sib])
        own = dot(mixed[h, me_v], weights[2, lanes(h), :])
        if h == 0:
            total[...] = own
        else:
            total[...] += own

    def far_part(h):
        value = acc[:, lanes(h)]
        for d in range(1, ny):
            src = y_from(d)
            value = value + dot(dense[src], mixed[h, src])
        for d in range(1, ny):
            src = ((y - d + ny) % ny) * 2 + 1 - core
            for g in range(GROUPS):
                block = mixed.at[h, src, group_rows(g)]
                remote(block, block, f4_send.at[d, h, g], f4_recv.at[d, h, g], me_s, sib).wait_recv()
            value = value + dot(dense[src], mixed[h, src])
        last = dot(value.astype(BF16), weights[3, lanes(h), :])
        if h + 1 < parts:
            total[...] += last
        else:
            out[0] = (total[...] + last).astype(BF16)

    loads[2].wait()
    loads[3].wait()
    all_left()
    for h in range(parts):
        pieces_left(h, p2_send.at[h])
    send_group(0, 0)
    send_group(0, 1)
    for h in range(parts):
        pass_group(h, 0)
        if h + 1 < parts:
            send_group(h + 1, 0)
        if h > 0:
            far_part(h - 1)
        pass_group(h, 1)
        if h + 1 < parts:
            send_group(h + 1, 1)
            pieces_left(h, p3_send.at[h])
        near_part(h)
    far_part(parts - 1)
    pieces_left(parts - 1, p3_send.at[parts - 1])
    all_left()


def shards(n, nv, features, tile_values, tile_column, tile_count, *rest):
    _, rows, width = features.shape
    _, per, slots, tile, _ = tile_values.shape
    ny = nv // 2
    parts, cols, _, piece_rows, piece_cols = cut(n, rows, width)
    taps = rest[2].shape[0]
    dma = pltpu.SemaphoreType.DMA
    hbm = pl.BlockSpec(memory_space=pltpu.HBM)
    hold = [pltpu.with_memory_space_constraint(x, pltpu.HBM) for x in (features, tile_values, tile_column, tile_count, *rest)]
    summed = pl.pallas_call(
        functools.partial(kernel, (n, nv, rows, width, slots, tile)),
        out_shape=jax.ShapeDtypeStruct((1, rows, width), BF16),
        in_specs=[hbm] * 9,
        out_specs=pl.BlockSpec(memory_space=pltpu.VMEM),
        scratch_shapes=[
            pltpu.SMEM((per, slots), jnp.int32),
            pltpu.SMEM((1, per), jnp.int32),
            pltpu.VMEM((rows, width), BF16),
            pltpu.VMEM((parts, nv, rows, cols), BF16),
            pltpu.VMEM((per, slots, tile, tile), BF16),
            pltpu.VMEM((nv, rows, rows), BF16),
            pltpu.VMEM((4, width, width), BF16),
            pltpu.VMEM((taps, width), F32),
            pltpu.VMEM((rows, width), F32),
            pltpu.VMEM((rows, width), F32),
            pltpu.VMEM((parts, rows, cols), BF16),
            pltpu.VMEM((parts, n, piece_rows, piece_cols), BF16),
            pltpu.VMEM((parts, n, piece_rows, piece_cols), BF16),
            pltpu.VMEM((parts, nv, rows, cols), BF16),
            dma((9,)),
            dma((parts,)),
            dma((parts,)),
            dma((ny, parts)),
            dma((ny, parts)),
            dma((ny, parts)),
            dma((ny, parts)),
            dma((parts,)),
            dma((parts,)),
            dma((parts,)),
            dma((parts, GROUPS)),
            dma((ny, parts, GROUPS)),
            dma((ny, parts, GROUPS)),
            dma((parts,)),
            dma((parts,)),
            dma((ny, parts, GROUPS)),
            dma((ny, parts, GROUPS)),
        ],
        compiler_params=pltpu.CompilerParams(
            collective_id=0, has_side_effects=True, vmem_limit_bytes=40 * 1024 * 1024
        ),
    )(*hold)
    return jnp.maximum(summed, 0)


def solution(mesh):
    n, nv = mesh.shape["snap"], mesh.shape["vert"]
    return jax.shard_map(
        functools.partial(shards, n, nv),
        mesh=mesh,
        in_specs=(
            P("snap", "vert", None),
            P("snap", "vert", None, None, None),
            P("snap", "vert", None),
            P("snap", "vert"),
            P(),
            P(),
            P(),
            P(),
            P(),
        ),
        out_specs=P("snap", "vert", None),
        check_vma=False,
    )
```
